256 devices in a mesh: dp: 32 (over x_lo, z, core), tensor: 8 (over x_hi, y).
Axes of the slice: x: 4 (x_hi: 2, x_lo: 2; x = x_hi * 2 + x_lo), y: 4, z: 8, core: 2. Of those that a mesh axis runs over, the one named last changes fastest.
Arguments:
- averaged_picture_features: bfloat16 [65536, 1536], P(('dp', 'tensor')), may hold values from -6 to 6
- averaged_caption_features: bfloat16 [65536, 1536], P(('dp', 'tensor')), may hold values from -6 to 6
- picture_projector_weights_array: bfloat16 [1536, 1536], P(None, 'tensor'), may hold values from -0.00390625 to 0.00390625
- caption_projector_weights: bfloat16 [1536, 1536], P(None, 'tensor'), may hold values from -0.00390625 to 0.00390625
- sharpness_coefficient: float32 [1], replicated, may hold values from 5 to 15
- offset_term: float32 [1], replicated, may hold values from -3 to -1
- step_mate_bitflags: int32 [4], replicated, may hold values from 0 to 4, as said below
Outputs:
- grad_image: float32 [65536, 1536], P(('dp', 'tensor'))
- grad_text: float32 [65536, 1536], P(('dp', 'tensor'))
- row_loss: float32 [65536], P(('dp', 'tensor'))
The draws below stay inside these ranges and needn't reach their ends.
Inputs may be any that keep to these rules, and one draw needn't show every extreme that they name: `step_mate_bitflags`: 4 distinct values; 0 and 4 are always among them.
All inputs are finite; a program needn't handle non-finite values.
Results may differ from the reference program's by a relative error of at most 0.0003.
Values may be sent and summed in bfloat16 or wider, within the bound.
A program may use at most 128 MiB of HBM per device.

```python
import math
import jax
import jax.numpy as jnp
from jax import lax

W = 1536
E = 1536
PAIRS_DEV = 256
ROUNDS = 4
LOG_DP = 5
PAIRS = 65536
N_DP = 32
N_TENSOR = 8


def draw_step_mate_bitflags(key, part):
    key = jax.random.fold_in(key, 7)
    skip_key, order_key = jax.random.split(key)
    skipped = jax.random.randint(skip_key, (), 1, LOG_DP - 1)
    shuffled = jax.random.permutation(order_key, jnp.arange(LOG_DP, dtype=jnp.int32))
    scores = jnp.where(shuffled == skipped, LOG_DP, jnp.arange(LOG_DP, dtype=jnp.int32))
    ranked = jnp.argsort(scores, stable=True)
    return jnp.take(shuffled, ranked[:ROUNDS]).astype(jnp.int32)


def steps_of(rng, dims, pieces, smallest, high):
    loudness = 1.0
    for dim, blocks in pieces:
        heights = jax.random.uniform(jax.random.fold_in(jax.random.fold_in(rng, 6), dim), (blocks,), jnp.float32, smallest / len(pieces), high / len(pieces))
        loudness = loudness * jnp.repeat(jnp.exp(heights), dims[dim] // blocks).reshape((-1,) + (1,) * (len(dims) - 1 - dim))
    return loudness


def noise(stream_key, shape, width, reach, pieces=(), kind=jnp.bfloat16):
    array = jax.random.normal(stream_key, shape, jnp.float32) * width
    if len(pieces) > 0:
        array = steps_of(stream_key, shape, pieces, -0.22, 0.18) * array
    return jnp.clip(array, min=-reach, max=reach).astype(kind)


def setup_inputs(seed: int = 0) -> dict:
    splits = jax.random.split(jax.random.key(seed), 8)
    return {
        "averaged_picture_features": noise(splits[0], (PAIRS, W), 1.0, 6.0, ((0, 256),)),
        "averaged_caption_features": noise(splits[1], (PAIRS, W), 1.0, 6.0, ((0, 256),)),
        "picture_projector_weights_array": noise(splits[2], (W, E), (W * E) ** -0.5, 0.00390625, ((1, 8),)),
        "caption_projector_weights": noise(splits[3], (W, E), (W * E) ** -0.5, 0.00390625, ((1, 8),)),
        "sharpness_coefficient": jnp.clip(jnp.exp(jax.random.uniform(splits[4], (1,), jnp.float32, math.log(5.0), math.log(15.0))), 5.0, 15.0),
        "offset_term": jnp.clip(jax.random.uniform(splits[5], (1,), jnp.float32, -3.0, -1.0), -3.0, -1.0),
        "step_mate_bitflags": draw_step_mate_bitflags(jax.random.fold_in(splits[7], 71), 0),
    }


highest = lax.Precision.HIGHEST

def normalize(embedding):
    inverse = lax.rsqrt(lax.optimization_barrier(jnp.sum(embedding * embedding, axis=-1)) + 1e-06)
    return (embedding * inverse[..., None], inverse)

def tile_terms(image_side, text_side, similarity_multiplier, logit_bias, labels):
    logits = similarity_multiplier * jnp.einsum('gtie,gtje->gtij', image_side, text_side, precision=highest) + logit_bias
    signed = labels * logits
    losses = lax.optimization_barrier(jnp.sum(jax.nn.softplus(-signed), axis=-1))
    weights = -labels * jax.nn.sigmoid(-signed) * similarity_multiplier
    return (losses, weights)

def backward_pass(grad_unit, embedding, inverse):
    radial = lax.optimization_barrier(jnp.sum(embedding * grad_unit, axis=-1))
    return inverse[:, None] * grad_unit - (inverse ** 3 * radial)[:, None] * embedding

def reference(averaged_picture_features, averaged_caption_features, picture_projector_weights_array, caption_projector_weights, sharpness_coefficient, offset_term, step_mate_bitflags):
    image_embed = jnp.dot(averaged_picture_features.astype(jnp.float32), picture_projector_weights_array.astype(jnp.float32), precision=highest, preferred_element_type=jnp.float32)
    text_embed = jnp.dot(averaged_caption_features.astype(jnp.float32), caption_projector_weights.astype(jnp.float32), precision=highest, preferred_element_type=jnp.float32)
    image_unit, image_inverse = normalize(image_embed)
    text_unit, text_inverse = normalize(text_embed)
    block_shape = (N_DP, N_TENSOR, PAIRS_DEV, E)
    image_block_list = image_unit.reshape(block_shape)
    text_blocks = text_unit.reshape(block_shape)
    similarity_multiplier = sharpness_coefficient[0]
    logit_bias = offset_term[0]
    own_labels = jnp.where(jnp.eye(PAIRS_DEV, dtype=bool), 1.0, -1.0).astype(jnp.float32)
    other_labels = -jnp.ones((PAIRS_DEV, PAIRS_DEV), jnp.float32)
    losses, weights = tile_terms(image_block_list, text_blocks, similarity_multiplier, logit_bias, own_labels)
    grad_image_unit = jnp.einsum('gtij,gtje->gtie', weights, text_blocks, precision=highest)
    grad_text_unit = jnp.einsum('gtij,gtie->gtje', weights, image_block_list, precision=highest)
    groups = jnp.arange(N_DP, dtype=jnp.int32)
    for round_index in range(ROUNDS):
        partner_index = jnp.bitwise_xor(groups, jnp.left_shift(jnp.int32(1), step_mate_bitflags[round_index]))
        partner = jnp.take(text_blocks, partner_index, axis=0)
        tile_loss, tile_weights = tile_terms(image_block_list, partner, similarity_multiplier, logit_bias, other_labels)
        losses = losses + tile_loss
        grad_image_unit = grad_image_unit + jnp.einsum('gtij,gtje->gtie', tile_weights, partner, precision=highest)
        returned = jnp.einsum('gtij,gtie->gtje', tile_weights, image_block_list, precision=highest)
        grad_text_unit = grad_text_unit + jnp.take(returned, partner_index, axis=0)
    grad_image = backward_pass(grad_image_unit.reshape(PAIRS, E), image_embed, image_inverse)
    grad_text = backward_pass(grad_text_unit.reshape(PAIRS, E), text_embed, text_inverse)
    row_loss = losses.reshape(PAIRS) / ((ROUNDS + 1) * PAIRS_DEV)
    return (grad_image, grad_text, row_loss)
```

```python
import functools

import jax
import jax.numpy as jnp
from jax import lax
from jax.experimental import pallas as pl
from jax.experimental.pallas import tpu as pltpu
from jax.sharding import PartitionSpec as P

MESH = pl.DeviceIdType.MESH
OWN, CORE, X_LO = 0, 2, 4
Z1 = (6, 8)
Z2 = (7, 9)
CHUNKS = 4
PARTS = 3


def flip(value, bit):
    size = 2**bit
    return value + size * (1 - 2 * ((value // size) % 2))


def dot(first, second):
    return jnp.dot(first, second, preferred_element_type=jnp.float32)


def dot_t(first, second):
    return lax.dot_general(
        first, second, (((1,), (1,)), ((), ())), preferred_element_type=jnp.float32
    )


def split(value):
    high = value.astype(jnp.bfloat16)
    low = (value - high.astype(jnp.float32)).astype(jnp.bfloat16)
    return high, low


def kernel(
    skip,
    image_ref,
    text_ref,
    image_w_ref,
    text_w_ref,
    scale_ref,
    bias_ref,
    grad_image_ref,
    grad_text_ref,
    loss_ref,
    feat,
    packed,
    rest,
    emb,
    inv,
    q_hi,
    q_lo,
    k_emb,
    k_hi,
    k_lo,
    grad,
    loss_acc,
    own_sem,
    send_sem,
    recv_sem,
    z1_send,
    z1_recv,
    z2_send,
    z2_recv,
    w_send,
    w_recv,
):
    rows, width = image_ref.shape
    shard = image_w_ref.shape[1]
    side = shard - 128
    half = width // 2
    dp = lax.axis_index("dp")
    tensor = lax.axis_index("tensor")
    core = dp % 2
    y = tensor % 4
    x_hi = tensor // 4

    def at(x_side, y_place):
        return x_side * 4 + (y_place + 4) % 4

    if skip == 1:
        z1_dp, z2_dp = flip(dp, 2), flip(flip(dp, 2), 3)
        near, far = z1_dp, z2_dp
    elif skip == 2:
        z1_dp, z2_dp = flip(dp, 1), flip(flip(dp, 1), 3)
    else:
        z1_dp, z2_dp = flip(dp, 1), flip(dp, 2)
    core_to = (flip(dp, 0), tensor)
    x_to = (flip(dp, 4), tensor)
    cross_to = (flip(dp, 4), at(1 - x_hi, y))
    up_to = (dp, at(x_hi, y + 1))
    down_to = (dp, at(x_hi, y - 1))
    z1_to = (z1_dp, tensor)
    z2_to = (z2_dp, tensor)

    barrier = pltpu.get_barrier_semaphore()
    peers = (core_to, x_to, cross_to, up_to, down_to, z1_to, z2_to)
    for peer in peers:
        pl.semaphore_signal(barrier, inc=1, device_id=peer, device_id_type=MESH)
    pl.semaphore_wait(barrier, len(peers))

    def remote(src, dst, send, recv, to):
        return pltpu.make_async_remote_copy(
            src_ref=src, dst_ref=dst, send_sem=send, recv_sem=recv, device_id=to, device_id_type=MESH
        )

    chunk_rows = rows // CHUNKS
    inputs = (image_ref, text_ref)

    def rows_of(j):
        return pl.ds((j % CHUNKS) * chunk_rows, chunk_rows)

    def z1_copy(j):
        kind, part = j // CHUNKS, rows_of(j)
        return remote(
            inputs[kind].at[part], feat.at[Z1[kind], part], z1_send.at[j], z1_recv.at[j], z1_to
        )

    def z2_copy(j):
        kind, part = j // CHUNKS, rows_of(j)
        source = inputs[kind].at[part] if skip == 3 else feat.at[Z1[kind], part]
        return remote(source, feat.at[Z2[kind], part], z2_send.at[j], z2_recv.at[j], z2_to)

    for j in range(2 * CHUNKS):
        z1_copy(j).start()
        if skip == 3:
            z2_copy(j).start()

    def whole_copy(kind, base, n, to):
        return remote(
            inputs[kind], feat.at[base + kind], send_sem.at[n], recv_sem.at[n], to
        )

    whole = [
        whole_copy(0, X_LO, 2, x_to),
        whole_copy(1, X_LO, 3, x_to),
        whole_copy(0, CORE, 0, core_to),
        whole_copy(1, CORE, 1, core_to),
    ]
    for copy in whole:
        copy.start()
    own = [pltpu.make_async_copy(inputs[k], feat.at[OWN + k], own_sem.at[k]) for k in range(2)]
    for copy in own:
        copy.start()

    even = tensor % 2 == 0
    for kind, w_ref in enumerate((image_w_ref, text_w_ref)):
        packed[kind, tensor, 0:width, :] = w_ref[:, 0:128]
        top = w_ref[0:half, 128:shard]
        bottom = w_ref[half:width, 128:shard]

        @pl.when(even)
        def _():
            packed[kind, tensor, width : width + half, :] = jnp.concatenate([top, bottom], axis=1)

        @pl.when(jnp.logical_not(even))
        def _():
            packed[kind, tensor, width : width + half, :] = jnp.concatenate([bottom, top], axis=1)

    depth = width + half
    all_rows = pl.ds(0, depth)
    first_rows = pl.ds(0, depth // 2)
    second_rows = pl.ds(depth // 2, depth // 2)
    own_slot = tensor
    below, above, opposite = at(x_hi, y - 1), at(x_hi, y + 1), at(x_hi, y + 2)
    cross = at(1 - x_hi, y)
    cross_below, cross_above, cross_opposite = (
        at(1 - x_hi, y - 1),
        at(1 - x_hi, y + 1),
        at(1 - x_hi, y + 2),
    )

    def shard_copy(kind, slot, part, send, recv, to):
        ref = packed.at[kind, slot, part]
        return remote(ref, ref, w_send.at[send], w_recv.at[recv], to)

    started = []

    def send(slot, part, number, recv, to):
        copy = shard_copy(core, slot, part, number, recv, to)
        copy.start()
        started.append(copy)

    def swap(number, slot):
        copy = shard_copy(core, slot, all_rows, 8 + number, 8 + number, core_to)
        copy.start()
        started.append(copy)

    def arrived(slot, part, recv):
        shard_copy(core, slot, part, recv, recv, core_to).wait_recv()

    send(own_slot, all_rows, 0, 0, up_to)
    send(own_slot, all_rows, 1, 1, down_to)
    send(own_slot, all_rows, 2, 2, cross_to)

    def relay(j):
        z1_copy(j).wait_recv()
        if skip != 3:
            z2_copy(j).start()

    relay(0)
    arrived(below, all_rows, 0)
    send(below, first_rows, 3, 3, up_to)
    arrived(above, all_rows, 1)
    send(above, second_rows, 4, 4, down_to)
    arrived(cross, all_rows, 2)
    send(cross, all_rows, 5, 5, up_to)
    send(cross, all_rows, 6, 6, down_to)
    swap(0, below)
    swap(1, above)
    swap(2, cross)
    relay(1)
    arrived(opposite, first_rows, 3)
    arrived(opposite, second_rows, 4)
    send(opposite, all_rows, 7, 7, cross_to)
    swap(3, opposite)
    relay(2)
    arrived(cross_below, all_rows, 5)
    swap(4, cross_below)
    arrived(cross_above, all_rows, 6)
    swap(5, cross_above)
    arrived(cross_opposite, all_rows, 7)
    swap(6, cross_opposite)
    relay(3)
    for number, slot in enumerate(
        (below, above, cross, opposite, cross_below, cross_above, cross_opposite)
    ):
        shard_copy(1 - core, slot, all_rows, 8 + number, 8 + number, core_to).wait_recv()

    low_lanes = lax.broadcasted_iota(jnp.int32, (half, 128), 1) < 64

    def unpack(n, _):
        kind, k = n // 4, n % 4
        left = packed[kind, 2 * k, width : width + half, :].astype(jnp.float32)
        right = packed[kind, 2 * k + 1, width : width + half, :].astype(jnp.float32)
        top = jnp.where(low_lanes, left, right)
        bottom = pltpu.roll(jnp.where(low_lanes, right, left), 64, 1)
        rest[kind, k, 0:half, :] = top.astype(jnp.bfloat16)
        rest[kind, k, half:width, :] = bottom.astype(jnp.bfloat16)
        return 0

    lax.fori_loop(0, 8, unpack, 0)

    tiles = width // 256
    main_tiles = 4

    def project(piece, kind, target):
        total = jnp.zeros((rows, 128), jnp.float32)
        for n in range(tiles):
            if n < main_tiles:
                right = jnp.concatenate(
                    [packed[kind, 2 * n, 0:width, :], packed[kind, 2 * n + 1, 0:width, :]], axis=1
                )
            else:
                k = 2 * (n - main_tiles)
                right = jnp.concatenate([rest[kind, k], rest[kind, k + 1]], axis=1)
            value = dot(feat[piece], right)
            target[:, n * 256 : (n + 1) * 256] = value
            square = value * value
            total = total + square[:, 0:128] + square[:, 128:256]
        return lax.rsqrt(jnp.sum(total, axis=-1, keepdims=True) + 1e-06)

    scale = scale_ref[0]
    bias = bias_ref[0]

    def side_terms(kind, keys_hi, keys_lo, diagonal):
        query = 1 - kind
        hi = keys_hi[...]
        inner = dot_t(q_hi[query], hi) + dot_t(q_hi[query], keys_lo[...]) + dot_t(q_lo[query], hi)
        logit = scale * inner + bias
        if diagonal:
            row = lax.broadcasted_iota(jnp.int32, logit.shape, 0)
            column = lax.broadcasted_iota(jnp.int32, logit.shape, 1)
            label = jnp.where(row == column, 1.0, -1.0).astype(jnp.float32)
            signed = -label * logit
            coef = (-label * scale) / (1.0 + jnp.exp(-signed))
        else:
            signed = logit
            coef = scale / (1.0 + jnp.exp(-signed))

        @pl.when(kind == 1)
        def _():
            loss = jnp.maximum(signed, 0.0) + jnp.log1p(jnp.exp(-jnp.abs(signed)))
            loss_acc[...] += loss[:, 0:128] + loss[:, 128:256]

        coef_hi, coef_lo = split(coef)
        for n in range(tiles):
            part = slice(n * 256, (n + 1) * 256)
            key = keys_hi[:, part]
            grad[query, :, part] += (
                dot(coef_hi, key) + dot(coef_hi, keys_lo[:, part]) + dot(coef_lo, key)
            )

    def units(source, factor, hi_ref, lo_ref):
        for n in range(tiles):
            part = slice(n * 256, (n + 1) * 256)
            hi_ref[:, part], lo_ref[:, part] = split(source[:, part] * factor)

    loss_acc[...] = jnp.zeros_like(loss_acc)
    grad[...] = jnp.zeros_like(grad)
    for copy in own:
        copy.wait()

    def own_units(kind, _):
        inverse = project(OWN + kind, kind, emb.at[kind])
        inv[kind] = jnp.broadcast_to(inverse, (rows, 128))
        units(emb.at[kind], inverse, q_hi.at[kind], q_lo.at[kind])
        return 0

    lax.fori_loop(0, 2, own_units, 0)

    def own_terms(kind, _):
        side_terms(kind, q_hi.at[kind], q_lo.at[kind], True)
        return 0

    lax.fori_loop(0, 2, own_terms, 0)

    def work(piece, kind):
        factor = project(piece, kind, k_emb)
        units(k_emb, factor, k_hi, k_lo)
        side_terms(kind, k_hi, k_lo, False)

    def work_step(piece, _):
        work(piece, jnp.where(piece < 6, piece % 2, piece // 2 - 3))
        return 0

    relay(4)
    whole[2].wait_recv()
    whole[3].wait_recv()
    lax.fori_loop(2, 4, work_step, 0)
    relay(5)
    whole[0].wait_recv()
    whole[1].wait_recv()
    lax.fori_loop(4, 6, work_step, 0)
    relay(6)
    for j in range(CHUNKS):
        z2_copy(j).wait_recv()
    lax.fori_loop(6, 8, work_step, 0)
    relay(7)
    for j in range(CHUNKS, 2 * CHUNKS):
        z2_copy(j).wait_recv()
    lax.fori_loop(8, 10, work_step, 0)

    low = lax.broadcasted_iota(jnp.int32, (rows, 128), 1) < 64
    for kind, out_ref in enumerate((grad_image_ref, grad_text_ref)):
        inverse = inv[kind]
        radial = jnp.zeros((rows, 128), jnp.float32)
        for n in range(width // 128):
            part = slice(n * 128, (n + 1) * 128)
            radial = radial + emb[kind, :, part] * grad[kind, :, part]
        radial = jnp.sum(radial, axis=-1, keepdims=True)
        factor = inverse * inverse * inverse * radial

        def out(n):
            part = slice(n * 128, (n + 1) * 128)
            return inverse * grad[kind, :, part] - factor * emb[kind, :, part]

        for k in range(4):
            first, second, third = out(2 * k), out(2 * k + 1), out(8 + k)
            turned = pltpu.roll(second, 64, 1)
            start = 384 * k
            out_ref[:, start : start + 128] = first
            out_ref[:, start + 128 : start + 256] = jnp.where(low, third, turned)
            out_ref[:, start + 256 : start + 384] = jnp.where(low, turned, third)
    loss_ref[...] = jnp.sum(loss_acc[...].T, axis=0, keepdims=True) / (5 * rows)

    for copy in whole:
        copy.wait_send()
    for j in range(2 * CHUNKS):
        z1_copy(j).wait_send()
        z2_copy(j).wait_send()
    for copy in started:
        copy.wait_send()


def run(skip, image, text, image_w, text_w, scale, bias):
    rows, width = image.shape
    depth = width + width // 2
    dma = pltpu.SemaphoreType.DMA
    f32, bf16 = jnp.float32, jnp.bfloat16
    any_spec = pl.BlockSpec(memory_space=pl.ANY)
    vmem = pl.BlockSpec(memory_space=pltpu.VMEM)
    smem = pl.BlockSpec(memory_space=pltpu.SMEM)
    grad_image, grad_text, loss = pl.pallas_call(
        functools.partial(kernel, skip),
        out_shape=(
            jax.ShapeDtypeStruct((rows, width), f32),
            jax.ShapeDtypeStruct((rows, width), f32),
            jax.ShapeDtypeStruct((1, rows), f32),
        ),
        in_specs=[any_spec, any_spec, vmem, vmem, smem, smem],
        out_specs=(vmem, vmem, vmem),
        scratch_shapes=[
            pltpu.VMEM((10, rows, width), bf16),
            pltpu.VMEM((2, 8, depth, 128), bf16),
            pltpu.VMEM((2, 4, width, 128), bf16),
            pltpu.VMEM((2, rows, width), f32),
            pltpu.VMEM((2, rows, 128), f32),
            pltpu.VMEM((2, rows, width), bf16),
            pltpu.VMEM((2, rows, width), bf16),
            pltpu.VMEM((rows, width), f32),
            pltpu.VMEM((rows, width), bf16),
            pltpu.VMEM((rows, width), bf16),
            pltpu.VMEM((2, rows, width), f32),
            pltpu.VMEM((rows, 128), f32),
            dma((2,)),
            dma((4,)),
            dma((4,)),
            dma((2 * CHUNKS,)),
            dma((2 * CHUNKS,)),
            dma((2 * CHUNKS,)),
            dma((2 * CHUNKS,)),
            dma((15,)),
            dma((15,)),
        ],
        compiler_params=pltpu.CompilerParams(
            collective_id=skip, has_side_effects=True, vmem_limit_bytes=56 * 2**20
        ),
    )(image, text, image_w, text_w, scale, bias)
    return grad_image, grad_text, loss.reshape(rows)


def body(image, text, image_w, text_w, scale, bias, flags):
    skip = 10 - jnp.sum(flags)
    return lax.switch(
        skip - 1,
        [functools.partial(run, 1), functools.partial(run, 2), functools.partial(run, 3)],
        image,
        text,
        image_w,
        text_w,
        scale,
        bias,
    )


def solution(mesh):
    placed = (
        P(("dp", "tensor"), None),
        P(("dp", "tensor"), None),
        P(None, "tensor"),
        P(None, "tensor"),
        P(),
        P(),
        P(),
    )
    return jax.shard_map(
        body,
        mesh=mesh,
        in_specs=placed,
        out_specs=(P(("dp", "tensor"), None), P(("dp", "tensor"), None), P(("dp", "tensor"))),
        check_vma=False,
    )
```

```python
import functools

import jax
import jax.numpy as jnp
from jax import lax
from jax.experimental import pallas as pl
from jax.experimental.pallas import tpu as pltpu
from jax.sharding import PartitionSpec as P

MESH = pl.DeviceIdType.MESH
OWN, CORE, X_LO, Z1, Z2 = 0, 1, 2, 3, 4
CHUNKS = 8
PIECES = 2 * CHUNKS
STEP = 3
AHEAD = 4


def flip(value, bit):
    size = 2**bit
    return value + size * (1 - 2 * ((value // size) % 2))


def dot(first, second):
    return jnp.dot(first, second, preferred_element_type=jnp.float32)


def dot_t(first, second):
    return lax.dot_general(
        first, second, (((1,), (1,)), ((), ())), preferred_element_type=jnp.float32
    )


def split(value):
    high = value.astype(jnp.bfloat16)
    low = (value - high.astype(jnp.float32)).astype(jnp.bfloat16)
    return high, low


def kernel(
    skip,
    image_ref,
    text_ref,
    image_w_ref,
    text_w_ref,
    scale_ref,
    bias_ref,
    grad_image_ref,
    grad_text_ref,
    loss_ref,
    feat,
    weights,
    emb,
    inv,
    inv_rows,
    totals,
    a_hi,
    a_lo,
    sums,
    hi,
    lo,
    loss_acc,
    out,
    own_sem,
    send_sem,
    recv_sem,
    z1_send,
    z1_recv,
    z2_send,
    z2_recv,
    w_send,
    w_recv,
    inv_send,
    inv_recv,
    out_sem,
):
    rows, width = image_ref.shape
    shard = image_w_ref.shape[0]
    dp = lax.axis_index("dp")
    tensor = lax.axis_index("tensor")
    core = dp % 2
    y = tensor % 4
    x_hi = tensor // 4

    def at(x_side, y_place):
        return x_side * 4 + (y_place + 4) % 4

    if skip == 1:
        z1_dp, far_dp = flip(dp, 2), flip(dp, 3)
        hop_dp = flip(flip(dp, 2), 3)
    elif skip == 2:
        z1_dp, far_dp = flip(dp, 1), flip(dp, 3)
        hop_dp = flip(flip(dp, 1), 3)
    else:
        z1_dp, far_dp = flip(dp, 1), flip(dp, 2)
        hop_dp = far_dp
    core_to = (flip(dp, 0), tensor)
    x_to = (flip(dp, 4), tensor)
    cross_to = (flip(dp, 4), at(1 - x_hi, y))
    up_to = (dp, at(x_hi, y + 1))
    down_to = (dp, at(x_hi, y - 1))
    z1_to = (z1_dp, tensor)
    hop_to = (hop_dp, tensor)
    far_to = (far_dp, tensor)

    barrier = pltpu.get_barrier_semaphore()
    peers = [core_to, x_to, cross_to, up_to, down_to, z1_to, hop_to]
    if skip != 3:
        peers.append(far_to)
    for peer in peers:
        pl.semaphore_signal(barrier, inc=1, device_id=peer, device_id_type=MESH)
    pl.semaphore_wait(barrier, len(peers))

    def remote(src, dst, send, recv, to):
        return pltpu.make_async_remote_copy(
            src_ref=src, dst_ref=dst, send_sem=send, recv_sem=recv, device_id=to, device_id_type=MESH
        )

    chunk_rows = rows // CHUNKS
    inputs = (image_ref, text_ref)
    def rows_of(j):
        return pl.ds(pl.multiple_of((j % CHUNKS) * chunk_rows, chunk_rows), chunk_rows)

    def z1_copy(j, source=None):
        landing = feat.at[Z1, j // CHUNKS, rows_of(j)]
        return remote(
            landing if source is None else source, landing, z1_send.at[j], z1_recv.at[j], z1_to
        )

    def z2_copy(j, source=None):
        source = feat.at[Z1, j // CHUNKS, rows_of(j)] if source is None else source
        landing = feat.at[Z2, j // CHUNKS, rows_of(j)]
        return remote(source, landing, z2_send.at[j], z2_recv.at[j], hop_to)

    def send_chunk(j, _, source=None):
        source = feat.at[OWN, j // CHUNKS, rows_of(j)] if source is None else source
        z1_copy(j, source).start()
        if skip == 3:
            z2_copy(j, source).start()
        return 0

    at_once = AHEAD if skip == 1 else PIECES
    lax.fori_loop(
        0, min(at_once, CHUNKS), lambda j, _: send_chunk(j, 0, image_ref.at[rows_of(j)]), 0
    )
    lax.fori_loop(
        CHUNKS, max(at_once, CHUNKS), lambda j, _: send_chunk(j, 0, text_ref.at[rows_of(j)]), 0
    )

    w_inputs = (image_w_ref, text_w_ref)
    shard_rows = (0, shard)
    first_rows = (0, shard // 2)
    second_rows = (shard // 2, shard // 2)
    below, above, opposite = at(x_hi, y - 1), at(x_hi, y + 1), at(x_hi, y + 2)
    cross = at(1 - x_hi, y)
    cross_below, cross_above, cross_opposite = (
        at(1 - x_hi, y - 1),
        at(1 - x_hi, y + 1),
        at(1 - x_hi, y + 2),
    )

    def place(kind, slot, part):
        offset = pl.multiple_of(slot * shard + part[0], shard // 2)
        return weights.at[kind, pl.ds(offset, part[1])]

    def shard_copy(kind, slot, part, send, recv, to):
        ref = place(kind, slot, part)
        return remote(ref, ref, w_send.at[send], w_recv.at[recv], to)

    def own_shard_copy(kind, number, to):
        return remote(
            w_inputs[kind],
            place(kind, tensor, shard_rows),
            w_send.at[number],
            w_recv.at[number],
            to,
        )

    own_targets = (up_to, down_to, cross_to)
    for kind in range(2):

        @pl.when(core == kind)
        def _():
            for number, to in enumerate(own_targets):
                own_shard_copy(kind, number, to).start()

    def whole_copy(kind, base, n, to):
        return remote(
            inputs[kind], feat.at[base, kind], send_sem.at[n], recv_sem.at[n], to
        )

    whole = [
        whole_copy(0, X_LO, 2, x_to),
        whole_copy(1, X_LO, 3, x_to),
        whole_copy(0, CORE, 0, core_to),
        whole_copy(1, CORE, 1, core_to),
    ]
    for copy in whole:
        copy.start()
    own = [pltpu.make_async_copy(inputs[k], feat.at[OWN, k], own_sem.at[k]) for k in range(2)]
    for kind in range(2):
        own.append(
            pltpu.make_async_copy(
                w_inputs[kind], place(kind, tensor, shard_rows), own_sem.at[2 + kind]
            )
        )
    for copy in own:
        copy.start()

    def send(slot, part, number, to):
        shard_copy(core, slot, part, number, number, to).start()

    def swap(number, slot):
        send(slot, shard_rows, 8 + number, core_to)

    def arrived(slot, part, recv):
        shard_copy(core, slot, part, recv, recv, core_to).wait_recv()

    def swapped(number, slot):
        shard_copy(1 - core, slot, shard_rows, 8 + number, 8 + number, core_to).wait_recv()

    def relay(first, last):
        def one(j, _):
            z1_copy(j).wait_recv()
            if skip != 3:
                z2_copy(j).start()
            if skip == 1:

                @pl.when(j + AHEAD < PIECES)
                def _():
                    send_chunk(j + AHEAD, 0)

            return 0

        lax.fori_loop(first, last, one, 0)

    def wait_z2(first, last):
        def one(j, _):
            z2_copy(j).wait_recv()
            return 0

        lax.fori_loop(first, last, one, 0)

    def early(first, last):
        if skip != 3:
            relay(first, last)

    tiles = width // 256

    def tile(n):
        return slice(n * 256, (n + 1) * 256)

    def over_tiles(body, carry):
        def several(m, carry):
            for k in range(STEP):
                carry = body(pl.ds(pl.multiple_of((m * STEP + k) * 256, 256), 256), carry)
            return carry

        return lax.fori_loop(0, tiles // STEP, several, carry)

    scale = scale_ref[0]
    bias = bias_ref[0]
    loss_acc[...] = jnp.zeros_like(loss_acc)
    sums[...] = jnp.zeros_like(sums)

    totals[...] = jnp.zeros_like(totals)
    out[...] = jnp.zeros_like(out)
    for copy in own:
        copy.wait()

    def group(g, _):
        @pl.when(g == 0)
        def _():
            early(0, 3)
            arrived(below, shard_rows, 0)
            arrived(above, shard_rows, 1)
            send(below, first_rows, 3, up_to)
            send(above, second_rows, 4, down_to)
            arrived(cross, shard_rows, 2)
            swap(0, below)
            swap(1, above)
            swap(2, cross)
            early(3, 4)
            arrived(opposite, first_rows, 3)
            arrived(opposite, second_rows, 4)
            send(cross, shard_rows, 5, up_to)
            send(cross, shard_rows, 6, down_to)
            send(opposite, shard_rows, 7, cross_to)
            swap(3, opposite)
            early(4, 5)
            swapped(0, below)
            swapped(1, above)
            swapped(3, opposite)

        @pl.when(g == 1)
        def _():
            early(6, 7)
            arrived(cross_below, shard_rows, 5)
            swap(4, cross_below)
            arrived(cross_above, shard_rows, 6)
            swap(5, cross_above)
            arrived(cross_opposite, shard_rows, 7)
            swap(6, cross_opposite)
            early(7, 8)
            swapped(2, cross)
            swapped(4, cross_below)
            swapped(5, cross_above)
            swapped(6, cross_opposite)

        side = x_hi + g * (1 - 2 * x_hi)
        begin = pl.multiple_of(side * (width // 2), width // 2)

        def embed(kind, _):
            def one(m, total):
                for k in range(STEP):
                    part = pl.ds(pl.multiple_of(begin + (m * STEP + k) * 256, 256), 256)
                    value = dot_t(feat[OWN, kind], weights[kind, part, :])
                    emb[kind, :, part] = value
                    square = value * value
                    total = total + square[:, 0:128] + square[:, 128:256]
                return total

            totals[kind] = lax.fori_loop(0, tiles // 2 // STEP, one, totals[kind])
            return 0

        lax.fori_loop(0, 2, embed, 0)
        early(5 + 3 * g, 6 + 3 * g)

        def through(kind, _):
            half = pl.ds(begin, width // 2)
            hi_half, lo_half = split(emb[1 - kind, :, half])

            def back(part, carry):
                right = weights[kind, half, part]
                out[kind, :, part] += dot(hi_half, right) + dot(lo_half, right)
                return carry

            over_tiles(back, 0)
            return 0

        lax.fori_loop(0, 2, through, 0)
        return 0

    lax.fori_loop(0, 2, group, 0)

    def inv_copy(n, base, to):
        return remote(inv_rows.at[OWN], inv_rows.at[base], inv_send.at[n], inv_recv.at[n], to)

    inv_copies = [
        inv_copy(2, Z1, z1_to),
        inv_copy(3, Z2, far_to),
        inv_copy(0, CORE, core_to),
        inv_copy(1, X_LO, x_to),
    ]

    for kind in range(2):
        inverse = lax.rsqrt(jnp.sum(totals[kind], axis=-1, keepdims=True) + 1e-06)
        wide = jnp.broadcast_to(inverse, (rows, 128))
        inv[kind] = wide
        inv_rows[OWN, kind] = wide.T[0:8]
    for copy in inv_copies:
        copy.start()

    def queries(kind, _):
        factor = inv[1 - kind][:, 0:1]
        for n in range(tiles):
            a_hi[kind, :, tile(n)], a_lo[kind, :, tile(n)] = split(out[kind, :, tile(n)] * factor)
        return 0

    lax.fori_loop(0, 2, queries, 0)

    def terms(block, kind):
        keys = feat[block, kind]
        inner = dot_t(a_hi[kind], keys) + dot_t(a_lo[kind], keys)
        factor = scale * inv_rows[block, kind, 0:1, :]
        logit = inner * factor + bias
        row = lax.broadcasted_iota(jnp.int32, logit.shape, 0)
        column = lax.broadcasted_iota(jnp.int32, logit.shape, 1)
        own_rows = jnp.where(block == OWN, rows, 0)
        sign = jnp.where((row == column) & (row < own_rows), -1.0, 1.0).astype(jnp.float32)
        signed = sign * logit
        coef = (sign * factor) / (1.0 + jnp.exp(-signed))

        @pl.when(kind == 1)
        def _():
            loss = jnp.maximum(signed, 0.0) + jnp.log1p(jnp.exp(-jnp.abs(signed)))
            loss_acc[...] += loss[:, 0:128] + loss[:, 128:256]

        coef_hi, coef_lo = split(coef)

        def add(part, carry):
            key = feat[block, kind, :, part]
            sums[kind, :, part] += dot(coef_hi, key) + dot(coef_lo, key)
            return carry

        over_tiles(add, 0)

    def finish(kind):
        query = 1 - kind
        for n in range(tiles):
            hi[:, tile(n)], lo[:, tile(n)] = split(sums[kind, :, tile(n)])

        def back(part, radial):
            right = weights[kind, part, :]
            value = dot_t(hi[...], right) + dot_t(lo[...], right)
            out[query, :, part] = value
            product = value * emb[query, :, part]
            return radial + product[:, 0:128] + product[:, 128:256]

        radial = over_tiles(back, jnp.zeros((rows, 128), jnp.float32))
        inverse = inv[query][:, 0:1]
        factor = inverse * inverse * inverse * jnp.sum(radial, axis=-1, keepdims=True)
        for n in range(tiles):
            out[query, :, tile(n)] = (
                inverse * out[query, :, tile(n)] - factor * emb[query, :, tile(n)]
            )

    first_end = 8

    def chunks_by(n):
        if skip == 3:
            return jnp.where(n < 6, 0, CHUNKS)
        return jnp.where(n < 0, 9, 9 + (n + 1) // 3)

    out_refs = (grad_image_ref, grad_text_ref)
    out_copies = [
        pltpu.make_async_copy(out.at[k], out_refs[k], out_sem.at[k]) for k in range(2)
    ]

    def step(n, _):
        relay(chunks_by(n - 1), chunks_by(n))

        @pl.when((n == first_end) | (n == 10))
        def _():
            finish(n // 10)

        for query, when in enumerate((10, first_end)):

            @pl.when(n == when)
            def _(query=query):
                out_copies[query].start()

        @pl.when(n == first_end)
        def _():
            relay(chunks_by(n), PIECES)

        @pl.when(n == 2)
        def _():
            for copy in whole[2:] + inv_copies[2:]:
                copy.wait_recv()

        @pl.when(n == 4)
        def _():
            for copy in whole[:2]:
                copy.wait_recv()

        @pl.when(n == 6)
        def _():
            for copy in inv_copies[:2]:
                copy.wait_recv()

        @pl.when(n == 7)
        def _():
            wait_z2(0, CHUNKS)

        @pl.when(n == 9)
        def _():
            wait_z2(CHUNKS, PIECES)

        block_z = Z1 + n % 2
        kind_z = (n - 6) // 2

        @pl.when(n < 10)
        def _():
            terms(jnp.where(n < 6, n // 2, block_z), jnp.where(n < 6, n % 2, kind_z))

        return 0

    lax.fori_loop(0, 11, step, 0)
    loss_ref[...] = jnp.sum(loss_acc[...].T, axis=0, keepdims=True) / (5 * rows)

    for copy in whole + inv_copies:
        copy.wait_send()

    def sent(j, _):
        z1_copy(j).wait_send()
        z2_copy(j).wait_send()
        return 0

    lax.fori_loop(0, PIECES, sent, 0)
    for copy in out_copies:
        copy.wait()
    for number, to in enumerate(own_targets):
        own_shard_copy(0, number, to).wait_send()
    for slot, part, number in (
        (below, first_rows, 3),
        (above, second_rows, 4),
        (cross, shard_rows, 5),
        (cross, shard_rows, 6),
        (opposite, shard_rows, 7),
    ):
        shard_copy(core, slot, part, number, number, core_to).wait_send()
    for number, slot in enumerate(
        (below, above, cross, opposite, cross_below, cross_above, cross_opposite)
    ):
        shard_copy(core, slot, shard_rows, 8 + number, 8 + number, core_to).wait_send()


def run(skip, image, text, image_w, text_w, scale, bias):
    rows, width = image.shape
    dma = pltpu.SemaphoreType.DMA
    f32, bf16 = jnp.float32, jnp.bfloat16
    any_spec = pl.BlockSpec(memory_space=pl.ANY)
    vmem = pl.BlockSpec(memory_space=pltpu.VMEM)
    smem = pl.BlockSpec(memory_space=pltpu.SMEM)
    grad_image, grad_text, loss = pl.pallas_call(
        functools.partial(kernel, skip),
        out_shape=(
            jax.ShapeDtypeStruct((rows, width), f32),
            jax.ShapeDtypeStruct((rows, width), f32),
            jax.ShapeDtypeStruct((1, rows), f32),
        ),
        in_specs=[any_spec, any_spec, any_spec, any_spec, smem, smem],
        out_specs=(any_spec, any_spec, vmem),
        scratch_shapes=[
            pltpu.VMEM((5, 2, rows, width), bf16),
            pltpu.VMEM((2, width, width), bf16),
            pltpu.VMEM((2, rows, width), f32),
            pltpu.VMEM((2, rows, 128), f32),
            pltpu.VMEM((5, 2, 8, rows), f32),
            pltpu.VMEM((2, rows, 128), f32),
            pltpu.VMEM((2, rows, width), bf16),
            pltpu.VMEM((2, rows, width), bf16),
            pltpu.VMEM((2, rows, width), f32),
            pltpu.VMEM((rows, width), bf16),
            pltpu.VMEM((rows, width), bf16),
            pltpu.VMEM((rows, 128), f32),
            pltpu.VMEM((2, rows, width), f32),
            dma((4,)),
            dma((4,)),
            dma((4,)),
            dma((2 * CHUNKS,)),
            dma((2 * CHUNKS,)),
            dma((2 * CHUNKS,)),
            dma((2 * CHUNKS,)),
            dma((15,)),
            dma((15,)),
            dma((4,)),
            dma((4,)),
            dma((2,)),
        ],
        compiler_params=pltpu.CompilerParams(
            collective_id=skip, has_side_effects=True, vmem_limit_bytes=48 * 2**20
        ),
    )(image, text, image_w.T, text_w.T, scale, bias)
    return grad_image, grad_text, loss


def body(image, text, image_w, text_w, scale, bias, flags):
    skip = 10 - jnp.sum(flags)
    grad_image, grad_text, loss = lax.switch(
        skip - 1,
        [functools.partial(run, 1), functools.partial(run, 2), functools.partial(run, 3)],
        image,
        text,
        image_w,
        text_w,
        scale,
        bias,
    )
    return grad_image, grad_text, loss.reshape(loss.shape[1])


def solution(mesh):
    placed = (
        P(("dp", "tensor"), None),
        P(("dp", "tensor"), None),
        P(None, "tensor"),
        P(None, "tensor"),
        P(),
        P(),
        P(),
    )
    return jax.shard_map(
        body,
        mesh=mesh,
        in_specs=placed,
        out_specs=(P(("dp", "tensor"), None), P(("dp", "tensor"), None), P(("dp", "tensor"))),
        check_vma=False,
    )
```

```python
import functools

import jax
import jax.numpy as jnp
from jax import lax
from jax.experimental import pallas as pl
from jax.experimental.pallas import tpu as pltpu
from jax.sharding import PartitionSpec as P

MESH = pl.DeviceIdType.MESH
OWN, CORE, X_LO, Z1, Z2 = 0, 1, 2, 3, 4
PARTS = 2
CHUNKS = 8
PIECES = 2 * CHUNKS
STEP = 3
AHEAD = 4


def flip(value, bit):
    size = 2**bit
    return value + size * (1 - 2 * ((value // size) % 2))


def dot(first, second):
    return jnp.dot(first, second, preferred_element_type=jnp.float32)


def dot_t(first, second):
    return lax.dot_general(
        first, second, (((1,), (1,)), ((), ())), preferred_element_type=jnp.float32
    )


def split(value):
    high = value.astype(jnp.bfloat16)
    low = (value - high.astype(jnp.float32)).astype(jnp.bfloat16)
    return high, low


def kernel(
    skip,
    image_ref,
    text_ref,
    image_w_ref,
    text_w_ref,
    scale_ref,
    bias_ref,
    grad_image_ref,
    grad_text_ref,
    loss_ref,
    feat,
    weights,
    emb,
    inv,
    inv_rows,
    totals,
    key_inv,
    radial_sums,
    a_hi,
    a_lo,
    sums,
    hi,
    lo,
    loss_acc,
    out,
    own_sem,
    send_sem,
    recv_sem,
    z1_send,
    z1_recv,
    z2_send,
    z2_recv,
    w_send,
    w_recv,
    inv_send,
    inv_recv,
    out_sem,
):
    rows, width = image_ref.shape
    shard = image_w_ref.shape[0]
    dp = lax.axis_index("dp")
    tensor = lax.axis_index("tensor")
    core = dp % 2
    y = tensor % 4
    x_hi = tensor // 4

    def at(x_side, y_place):
        return x_side * 4 + (y_place + 4) % 4

    if skip == 1:
        z1_dp, far_dp = flip(dp, 2), flip(dp, 3)
        hop_dp = flip(flip(dp, 2), 3)
    elif skip == 2:
        z1_dp, far_dp = flip(dp, 1), flip(dp, 3)
        hop_dp = flip(flip(dp, 1), 3)
    else:
        z1_dp, far_dp = flip(dp, 1), flip(dp, 2)
        hop_dp = far_dp
    core_to = (flip(dp, 0), tensor)
    x_to = (flip(dp, 4), tensor)
    cross_to = (flip(dp, 4), at(1 - x_hi, y))
    up_to = (dp, at(x_hi, y + 1))
    down_to = (dp, at(x_hi, y - 1))
    z1_to = (z1_dp, tensor)
    hop_to = (hop_dp, tensor)
    far_to = (far_dp, tensor)

    barrier = pltpu.get_barrier_semaphore()
    peers = [core_to, x_to, cross_to, up_to, down_to, z1_to, hop_to]
    if skip != 3:
        peers.append(far_to)
    for peer in peers:
        pl.semaphore_signal(barrier, inc=1, device_id=peer, device_id_type=MESH)
    pl.semaphore_wait(barrier, len(peers))

    def remote(src, dst, send, recv, to):
        return pltpu.make_async_remote_copy(
            src_ref=src, dst_ref=dst, send_sem=send, recv_sem=recv, device_id=to, device_id_type=MESH
        )

    chunk_rows = rows // CHUNKS
    inputs = (image_ref, text_ref)
    def rows_of(j):
        return pl.ds(pl.multiple_of((j % CHUNKS) * chunk_rows, chunk_rows), chunk_rows)

    per_part = CHUNKS // PARTS
    part_rows = rows // PARTS

    def landing(far, j):
        k = j - CHUNKS
        image = (6 + far) * rows + j * chunk_rows
        text = 8 * rows + (2 * (k // per_part) + far) * part_rows
        text = text + (k % per_part) * chunk_rows
        start = jnp.where(j < CHUNKS, image, text)
        return feat.at[pl.ds(pl.multiple_of(start, chunk_rows), chunk_rows)]

    def z1_copy(j, source=None):
        place = landing(0, j)
        return remote(
            place if source is None else source, place, z1_send.at[j], z1_recv.at[j], z1_to
        )

    def z2_copy(j, source=None):
        source = landing(0, j) if source is None else source
        return remote(source, landing(1, j), z2_send.at[j], z2_recv.at[j], hop_to)

    def send_chunk(j, _, source=None):
        source = feat.at[pl.ds(pl.multiple_of(j * chunk_rows, chunk_rows), chunk_rows)] if source is None else source
        z1_copy(j, source).start()
        if skip == 3:
            z2_copy(j, source).start()
        return 0

    lax.fori_loop(0, AHEAD, lambda j, _: send_chunk(j, 0, image_ref.at[rows_of(j)]), 0)

    w_inputs = (image_w_ref, text_w_ref)
    shard_rows = (0, shard)
    first_rows = (0, shard // 2)
    second_rows = (shard // 2, shard // 2)
    below, above, opposite = at(x_hi, y - 1), at(x_hi, y + 1), at(x_hi, y + 2)
    cross = at(1 - x_hi, y)
    cross_below, cross_above, cross_opposite = (
        at(1 - x_hi, y - 1),
        at(1 - x_hi, y + 1),
        at(1 - x_hi, y + 2),
    )

    def place(kind, slot, part):
        offset = pl.multiple_of(slot * shard + part[0], shard // 2)
        return weights.at[kind, pl.ds(offset, part[1])]

    def shard_copy(kind, slot, part, send, recv, to):
        ref = place(kind, slot, part)
        return remote(ref, ref, w_send.at[send], w_recv.at[recv], to)

    def own_shard_copy(kind, number, to):
        return remote(
            w_inputs[kind],
            place(kind, tensor, shard_rows),
            w_send.at[number],
            w_recv.at[number],
            to,
        )

    own_targets = (up_to, down_to, cross_to)
    for kind in range(2):

        @pl.when(core == kind)
        def _():
            for number, to in enumerate(own_targets):
                own_shard_copy(kind, number, to).start()

    def piece(n):
        return feat.at[pl.ds(pl.multiple_of(n * rows, rows), rows)]

    def whole_copy(kind, base, n, to):
        return remote(
            inputs[kind], piece(2 * base + kind), send_sem.at[n], recv_sem.at[n], to
        )

    whole = [
        whole_copy(0, X_LO, 2, x_to),
        whole_copy(1, X_LO, 3, x_to),
        whole_copy(0, CORE, 0, core_to),
        whole_copy(1, CORE, 1, core_to),
    ]
    for copy in whole:
        copy.start()
    own = [pltpu.make_async_copy(inputs[k], piece(k), own_sem.at[k]) for k in range(2)]
    for kind in range(2):
        own.append(
            pltpu.make_async_copy(
                w_inputs[kind], place(kind, tensor, shard_rows), own_sem.at[2 + kind]
            )
        )
    for copy in own:
        copy.start()

    def send(slot, part, number, to):
        shard_copy(core, slot, part, number, number, to).start()

    def swap(number, slot):
        send(slot, shard_rows, 8 + number, core_to)

    def arrived(slot, part, recv):
        shard_copy(core, slot, part, recv, recv, core_to).wait_recv()

    def swapped(number, slot):
        shard_copy(1 - core, slot, shard_rows, 8 + number, 8 + number, core_to).wait_recv()

    def relay(first, last):
        def one(j, _):
            z1_copy(j).wait_recv()
            if skip != 3:
                z2_copy(j).start()

            @pl.when(j + AHEAD < PIECES)
            def _():
                send_chunk(j + AHEAD, 0)

            return 0

        lax.fori_loop(first, last, one, 0)

    def wait_z2(first, last):
        def one(j, _):
            z2_copy(j).wait_recv()
            return 0

        lax.fori_loop(first, last, one, 0)

    tiles = width // 256

    def tile(n):
        return slice(n * 256, (n + 1) * 256)

    def over_tiles(body, carry):
        def several(m, carry):
            for k in range(STEP):
                carry = body(pl.ds(pl.multiple_of((m * STEP + k) * 256, 256), 256), carry)
            return carry

        return lax.fori_loop(0, tiles // STEP, several, carry)

    scale = scale_ref[0]
    bias = bias_ref[0]
    loss_acc[...] = jnp.zeros_like(loss_acc)
    sums[...] = jnp.zeros_like(sums)

    totals[...] = jnp.zeros_like(totals)
    out[...] = jnp.zeros_like(out)
    for copy in own:
        copy.wait()

    def group(g, _):
        @pl.when(g == 0)
        def _():
            relay(0, 3)
            arrived(below, shard_rows, 0)
            arrived(above, shard_rows, 1)
            send(below, first_rows, 3, up_to)
            send(above, second_rows, 4, down_to)
            arrived(cross, shard_rows, 2)
            swap(0, below)
            swap(1, above)
            swap(2, cross)
            relay(3, 4)
            arrived(opposite, first_rows, 3)
            arrived(opposite, second_rows, 4)
            send(cross, shard_rows, 5, up_to)
            send(cross, shard_rows, 6, down_to)
            send(opposite, shard_rows, 7, cross_to)
            swap(3, opposite)
            relay(4, 5)
            swapped(0, below)
            swapped(1, above)
            swapped(3, opposite)

        @pl.when(g == 1)
        def _():
            relay(6, 7)
            arrived(cross_below, shard_rows, 5)
            swap(4, cross_below)
            arrived(cross_above, shard_rows, 6)
            swap(5, cross_above)
            arrived(cross_opposite, shard_rows, 7)
            swap(6, cross_opposite)
            relay(7, 8)
            swapped(2, cross)
            swapped(4, cross_below)
            swapped(5, cross_above)
            swapped(6, cross_opposite)

        side = x_hi + g * (1 - 2 * x_hi)
        begin = pl.multiple_of(side * (width // 2), width // 2)

        def embed(kind, _):
            def one(m, total):
                for k in range(STEP):
                    part = pl.ds(pl.multiple_of(begin + (m * STEP + k) * 256, 256), 256)
                    value = dot_t(piece(kind)[...], weights[kind, part, :])
                    emb[kind, :, part] = value
                    square = value * value
                    total = total + square[:, 0:128] + square[:, 128:256]
                return total

            totals[kind] = lax.fori_loop(0, tiles // 2 // STEP, one, totals[kind])
            return 0

        lax.fori_loop(0, 2, embed, 0)
        relay(5 + 3 * g, 6 + 3 * g)

        def through(kind, _):
            half = pl.ds(begin, width // 2)
            hi_half, lo_half = split(emb[1 - kind, :, half])

            def back(part, carry):
                right = weights[kind, half, part]
                out[kind, :, part] += dot(hi_half, right) + dot(lo_half, right)
                return carry

            over_tiles(back, 0)
            return 0

        lax.fori_loop(0, 2, through, 0)
        return 0

    lax.fori_loop(0, 2, group, 0)

    def inv_copy(n, base, to):
        return remote(inv_rows.at[OWN], inv_rows.at[base], inv_send.at[n], inv_recv.at[n], to)

    inv_copies = [
        inv_copy(2, Z1, z1_to),
        inv_copy(3, Z2, far_to),
        inv_copy(0, CORE, core_to),
        inv_copy(1, X_LO, x_to),
    ]

    for kind in range(2):
        inverse = lax.rsqrt(jnp.sum(totals[kind], axis=-1, keepdims=True) + 1e-06)
        wide = jnp.broadcast_to(inverse, (rows, 128))
        inv[kind] = wide
        inv_rows[OWN, kind] = wide.T[0:8]
    for copy in inv_copies:
        copy.start()

    def queries(kind, _):
        factor = inv[1 - kind][:, 0:1]
        for n in range(tiles):
            a_hi[kind, :, tile(n)], a_lo[kind, :, tile(n)] = split(out[kind, :, tile(n)] * factor)
        return 0

    lax.fori_loop(0, 2, queries, 0)

    def coefs(keys, kind, inverses, diagonal):
        keys = keys[...]
        inner = dot_t(a_hi[kind], keys) + dot_t(a_lo[kind], keys)
        factor = scale * inverses
        logit = inner * factor + bias
        row = lax.broadcasted_iota(jnp.int32, logit.shape, 0)
        column = lax.broadcasted_iota(jnp.int32, logit.shape, 1)
        label_rows = jnp.where(diagonal, rows, 0)
        sign = jnp.where((row == column) & (row < label_rows), -1.0, 1.0).astype(jnp.float32)
        signed = sign * logit
        coef = (sign * factor) / (1.0 + jnp.exp(-signed))

        @pl.when(kind == 1)
        def _():
            loss = jnp.maximum(signed, 0.0) + jnp.log1p(jnp.exp(-jnp.abs(signed)))
            loss_acc[...] += loss[:, 0:128] + loss[:, 128:256]

        return split(coef)

    def add_terms(keys, kind, coef_hi, coef_lo):
        def add(part, carry):
            key = keys[:, part]
            sums[kind, :, part] += dot(coef_hi, key) + dot(coef_lo, key)
            return carry

        over_tiles(add, 0)

    def out_of_space(kind):
        for n in range(tiles):
            hi[:, tile(n)], lo[:, tile(n)] = split(sums[kind, :, tile(n)])

        def back(part, radial):
            right = weights[kind, part, :]
            value = dot_t(hi[...], right) + dot_t(lo[...], right)
            out[1 - kind, :, part] = value
            product = value * emb[1 - kind, :, part]
            return radial + product[:, 0:128] + product[:, 128:256]

        radial_sums[...] = over_tiles(back, jnp.zeros((rows, 128), jnp.float32))

    out_refs = (grad_image_ref, grad_text_ref)
    out_copies = [pltpu.make_async_copy(out.at[k], out_refs[k], out_sem.at[k]) for k in range(2)]

    def finish(query):
        inverse = inv[query][:, 0:1]
        radial = jnp.sum(radial_sums[...], axis=-1, keepdims=True)
        factor = inverse * inverse * inverse * radial
        for n in range(tiles):
            out[query, :, tile(n)] = (
                inverse * out[query, :, tile(n)] - factor * emb[query, :, tile(n)]
            )
        for k in range(2):

            @pl.when(query == k)
            def _(k=k):
                out_copies[k].start()

    before_finish = 14

    def chunks_by(n):
        return jnp.where(n < 0, 9, jnp.where(n < 8, 9 + (n + 1) // 2, jnp.where(n < 9, 15, PIECES)))

    def key_norms(keys, kind):
        def one(part, total):
            value = dot_t(keys[...], weights[kind, part, :])
            square = value * value
            return total + square[:, 0:128] + square[:, 128:256]

        total = over_tiles(one, jnp.zeros((rows, 128), jnp.float32))
        inverse = lax.rsqrt(jnp.sum(total, axis=-1, keepdims=True) + 1e-06)
        key_inv[...] = jnp.broadcast_to(inverse, (rows, 128)).T[0:8]

    def last_inverses():
        for copy in inv_copies[:2]:
            copy.wait_recv()
        for k, block in enumerate((Z1, Z2)):
            key_inv[:, k * part_rows : (k + 1) * part_rows] = inv_rows[
                block, 1, :, rows - part_rows : rows
            ]

    def step(n, _):
        relay(jnp.where(n == 8, before_finish, chunks_by(n - 1)), chunks_by(n))

        @pl.when(n == 2)
        def _():
            for copy in whole[2:] + inv_copies[2:]:
                copy.wait_recv()

        @pl.when(n == 4)
        def _():
            for copy in whole[:2]:
                copy.wait_recv()

        @pl.when(n == 7)
        def _():
            wait_z2(0, CHUNKS)

        @pl.when(n >= 8)
        def _():
            wait_z2(CHUNKS + (n - 8) * per_part, CHUNKS + (n - 7) * per_part)

        kind = jnp.where(n < 6, n % 2, n // 8)
        keys = piece(n)

        @pl.when((n >= 6) & (n < 9))
        def _():
            key_norms(keys, kind)

        @pl.when(n == 9)
        def _():
            last_inverses()

        known = inv_rows[jnp.minimum(n // 2, X_LO), kind, 0:1, :]
        inverses = jnp.where(n < 6, known, key_inv[0:1, :])
        coef_hi, coef_lo = coefs(keys, kind, inverses, n < 2)
        add_terms(keys, kind, coef_hi, coef_lo)
        return 0

    def phase(kind, _):
        lax.fori_loop(8 * kind, 8 + 2 * kind, step, 0)

        @pl.when(kind == 0)
        def _():
            relay(chunks_by(7), before_finish)

        out_of_space(kind)
        finish(1 - kind)
        return 0

    lax.fori_loop(0, 2, phase, 0)
    loss_ref[...] = jnp.sum(loss_acc[...].T, axis=0, keepdims=True) / (5 * rows)

    for copy in whole + inv_copies:
        copy.wait_send()

    def sent(j, _):
        z1_copy(j).wait_send()
        z2_copy(j).wait_send()
        return 0

    lax.fori_loop(0, PIECES, sent, 0)
    for copy in out_copies:
        copy.wait()
    for number, to in enumerate(own_targets):
        own_shard_copy(0, number, to).wait_send()
    for slot, part, number in (
        (below, first_rows, 3),
        (above, second_rows, 4),
        (cross, shard_rows, 5),
        (cross, shard_rows, 6),
        (opposite, shard_rows, 7),
    ):
        shard_copy(core, slot, part, number, number, core_to).wait_send()
    for number, slot in enumerate(
        (below, above, cross, opposite, cross_below, cross_above, cross_opposite)
    ):
        shard_copy(core, slot, shard_rows, 8 + number, 8 + number, core_to).wait_send()


def run(skip, image, text, image_w, text_w, scale, bias):
    rows, width = image.shape
    dma = pltpu.SemaphoreType.DMA
    f32, bf16 = jnp.float32, jnp.bfloat16
    any_spec = pl.BlockSpec(memory_space=pl.ANY)
    vmem = pl.BlockSpec(memory_space=pltpu.VMEM)
    smem = pl.BlockSpec(memory_space=pltpu.SMEM)
    grad_image, grad_text, loss = pl.pallas_call(
        functools.partial(kernel, skip),
        out_shape=(
            jax.ShapeDtypeStruct((rows, width), f32),
            jax.ShapeDtypeStruct((rows, width), f32),
            jax.ShapeDtypeStruct((1, rows), f32),
        ),
        in_specs=[any_spec, any_spec, any_spec, any_spec, smem, smem],
        out_specs=(any_spec, any_spec, vmem),
        scratch_shapes=[
            pltpu.VMEM((10 * rows, width), bf16),
            pltpu.VMEM((2, width, width), bf16),
            pltpu.VMEM((2, rows, width), f32),
            pltpu.VMEM((2, rows, 128), f32),
            pltpu.VMEM((5, 2, 8, rows), f32),
            pltpu.VMEM((2, rows, 128), f32),
            pltpu.VMEM((8, rows), f32),
            pltpu.VMEM((rows, 128), f32),
            pltpu.VMEM((2, rows, width), bf16),
            pltpu.VMEM((2, rows, width), bf16),
            pltpu.VMEM((2, rows, width), f32),
            pltpu.VMEM((rows, width), bf16),
            pltpu.VMEM((rows, width), bf16),
            pltpu.VMEM((rows, 128), f32),
            pltpu.VMEM((2, rows, width), f32),
            dma((4,)),
            dma((4,)),
            dma((4,)),
            dma((2 * CHUNKS,)),
            dma((2 * CHUNKS,)),
            dma((2 * CHUNKS,)),
            dma((2 * CHUNKS,)),
            dma((15,)),
            dma((15,)),
            dma((4,)),
            dma((4,)),
            dma((2,)),
        ],
        compiler_params=pltpu.CompilerParams(
            collective_id=skip, has_side_effects=True, vmem_limit_bytes=48 * 2**20
        ),
    )(image, text, image_w.T, text_w.T, scale, bias)
    return grad_image, grad_text, loss


def body(image, text, image_w, text_w, scale, bias, flags):
    skip = 10 - jnp.sum(flags)
    grad_image, grad_text, loss = lax.switch(
        skip - 1,
        [functools.partial(run, 1), functools.partial(run, 2), functools.partial(run, 3)],
        image,
        text,
        image_w,
        text_w,
        scale,
        bias,
    )
    return grad_image, grad_text, loss.reshape(loss.shape[1])


def solution(mesh):
    placed = (
        P(("dp", "tensor"), None),
        P(("dp", "tensor"), None),
        P(None, "tensor"),
        P(None, "tensor"),
        P(),
        P(),
        P(),
    )
    return jax.shard_map(
        body,
        mesh=mesh,
        in_specs=placed,
        out_specs=(P(("dp", "tensor"), None), P(("dp", "tensor"), None), P(("dp", "tensor"))),
        check_vma=False,
    )
```

```python
import functools

import jax
import jax.numpy as jnp
from jax import lax
from jax.experimental import pallas as pl
from jax.experimental.pallas import tpu as pltpu
from jax.sharding import PartitionSpec as P

MESH = pl.DeviceIdType.MESH
OWN, CORE, X_LO, Z1, Z2 = 0, 1, 2, 3, 4
PARTS = 2
CHUNKS = 8
PIECES = 2 * CHUNKS
STEP = 3
AHEAD = {1: 3, 2: 4, 3: 4}
PASSED = {1: (3, 4, 5, 6, 7, 8, 9), 2: (3, 5, 6, 7, 8, 9, 10), 3: (3, 4, 5, 6, 7, 8, 9)}


def flip(value, bit):
    size = 2**bit
    return value + size * (1 - 2 * ((value // size) % 2))


def dot(first, second):
    return jnp.dot(first, second, preferred_element_type=jnp.float32)


def dot_t(first, second):
    return lax.dot_general(
        first, second, (((1,), (1,)), ((), ())), preferred_element_type=jnp.float32
    )


def split(value):
    high = value.astype(jnp.bfloat16)
    low = (value - high.astype(jnp.float32)).astype(jnp.bfloat16)
    return high, low


def kernel(
    skip,
    image_ref,
    text_ref,
    image_w_ref,
    text_w_ref,
    scale_ref,
    bias_ref,
    grad_image_ref,
    grad_text_ref,
    loss_ref,
    feat,
    weights,
    emb,
    inv,
    inv_rows,
    totals,
    key_inv,
    radial_sums,
    a_hi,
    a_lo,
    sums,
    hi,
    lo,
    loss_acc,
    out,
    own_sem,
    send_sem,
    recv_sem,
    z1_send,
    z1_recv,
    z2_send,
    z2_recv,
    w_send,
    w_recv,
    inv_send,
    inv_recv,
):
    rows, width = image_ref.shape
    shard = image_w_ref.shape[0]
    dp = lax.axis_index("dp")
    tensor = lax.axis_index("tensor")
    core = dp % 2
    y = tensor % 4
    x_hi = tensor // 4

    def at(x_side, y_place):
        return x_side * 4 + (y_place + 4) % 4

    if skip == 1:
        z1_dp, far_dp = flip(dp, 2), flip(dp, 3)
        hop_dp = flip(flip(dp, 2), 3)
    elif skip == 2:
        z1_dp, far_dp = flip(dp, 1), flip(dp, 3)
        hop_dp = flip(flip(dp, 1), 3)
    else:
        z1_dp, far_dp = flip(dp, 1), flip(dp, 2)
        hop_dp = far_dp
    core_to = (flip(dp, 0), tensor)
    x_to = (flip(dp, 4), tensor)
    cross_to = (flip(dp, 4), at(1 - x_hi, y))
    up_to = (dp, at(x_hi, y + 1))
    down_to = (dp, at(x_hi, y - 1))
    z1_to = (z1_dp, tensor)
    hop_to = (hop_dp, tensor)
    far_to = (far_dp, tensor)

    barrier = pltpu.get_barrier_semaphore()
    peers = [core_to, x_to, cross_to, up_to, down_to, z1_to, hop_to]
    if skip != 3:
        peers.append(far_to)
    for peer in peers:
        pl.semaphore_signal(barrier, inc=1, device_id=peer, device_id_type=MESH)
    pl.semaphore_wait(barrier, len(peers))

    def remote(src, dst, send, recv, to):
        return pltpu.make_async_remote_copy(
            src_ref=src, dst_ref=dst, send_sem=send, recv_sem=recv, device_id=to, device_id_type=MESH
        )

    chunk_rows = rows // CHUNKS
    inputs = (image_ref, text_ref)
    def rows_of(j):
        return pl.ds(pl.multiple_of((j % CHUNKS) * chunk_rows, chunk_rows), chunk_rows)

    per_part = CHUNKS // PARTS
    part_rows = rows // PARTS

    def landing(far, j):
        k = j - CHUNKS
        image = (6 + far) * rows + j * chunk_rows
        text = 8 * rows + (2 * (k // per_part) + far) * part_rows
        text = text + (k % per_part) * chunk_rows
        start = jnp.where(j < CHUNKS, image, text)
        return feat.at[pl.ds(pl.multiple_of(start, chunk_rows), chunk_rows)]

    def z1_copy(j, source=None):
        place = landing(0, j)
        return remote(
            place if source is None else source, place, z1_send.at[j], z1_recv.at[j], z1_to
        )

    def z2_copy(j, source=None):
        source = landing(0, j) if source is None else source
        return remote(source, landing(1, j), z2_send.at[j], z2_recv.at[j], hop_to)

    def send_chunk(j, _, source=None):
        source = feat.at[pl.ds(pl.multiple_of(j * chunk_rows, chunk_rows), chunk_rows)] if source is None else source
        z1_copy(j, source).start()
        if skip == 3:
            z2_copy(j, source).start()
        return 0

    ahead = AHEAD[skip]
    passed = PASSED[skip]
    lax.fori_loop(0, ahead, lambda j, _: send_chunk(j, 0, image_ref.at[rows_of(j)]), 0)

    w_inputs = (image_w_ref, text_w_ref)
    shard_rows = (0, shard)
    first_rows = (0, shard // 2)
    second_rows = (shard // 2, shard // 2)
    below, above, opposite = at(x_hi, y - 1), at(x_hi, y + 1), at(x_hi, y + 2)
    cross = at(1 - x_hi, y)
    cross_below, cross_above, cross_opposite = (
        at(1 - x_hi, y - 1),
        at(1 - x_hi, y + 1),
        at(1 - x_hi, y + 2),
    )

    def place(kind, slot, part):
        offset = pl.multiple_of(slot * shard + part[0], shard // 2)
        return weights.at[kind, pl.ds(offset, part[1])]

    def shard_copy(kind, slot, part, send, recv, to):
        ref = place(kind, slot, part)
        return remote(ref, ref, w_send.at[send], w_recv.at[recv], to)

    def own_shard_copy(kind, number, to):
        return remote(
            w_inputs[kind],
            place(kind, tensor, shard_rows),
            w_send.at[number],
            w_recv.at[number],
            to,
        )

    own_targets = (up_to, down_to, cross_to)
    for kind in range(2):

        @pl.when(core == kind)
        def _():
            for number, to in enumerate(own_targets):
                own_shard_copy(kind, number, to).start()

    def piece(n):
        return feat.at[pl.ds(pl.multiple_of(n * rows, rows), rows)]

    def whole_copy(kind, base, n, to):
        return remote(
            inputs[kind], piece(2 * base + kind), send_sem.at[n], recv_sem.at[n], to
        )

    whole = [
        whole_copy(0, X_LO, 2, x_to),
        whole_copy(1, X_LO, 3, x_to),
        whole_copy(0, CORE, 0, core_to),
        whole_copy(1, CORE, 1, core_to),
    ]
    for copy in whole:
        copy.start()
    own = [pltpu.make_async_copy(inputs[k], piece(k), own_sem.at[k]) for k in range(2)]
    for kind in range(2):
        own.append(
            pltpu.make_async_copy(
                w_inputs[kind], place(kind, tensor, shard_rows), own_sem.at[2 + kind]
            )
        )
    for copy in own:
        copy.start()

    def send(slot, part, number, to):
        shard_copy(core, slot, part, number, number, to).start()

    def swap(number, slot):
        send(slot, shard_rows, 8 + number, core_to)

    def arrived(slot, part, recv):
        shard_copy(core, slot, part, recv, recv, core_to).wait_recv()

    def swapped(number, slot):
        shard_copy(1 - core, slot, shard_rows, 8 + number, 8 + number, core_to).wait_recv()

    def relay(first, last):
        def one(j, _):
            z1_copy(j).wait_recv()
            if skip != 3:
                z2_copy(j).start()

            @pl.when(j + ahead < PIECES)
            def _():
                send_chunk(j + ahead, 0)

            return 0

        lax.fori_loop(first, last, one, 0)

    def wait_z2(first, last):
        def one(j, _):
            z2_copy(j).wait_recv()
            return 0

        lax.fori_loop(first, last, one, 0)

    tiles = width // 256

    def tile(n):
        return slice(n * 256, (n + 1) * 256)

    def over_tiles(body, carry):
        def several(m, carry):
            for k in range(STEP):
                carry = body(pl.ds(pl.multiple_of((m * STEP + k) * 256, 256), 256), carry)
            return carry

        return lax.fori_loop(0, tiles // STEP, several, carry)

    scale = scale_ref[0]
    bias = bias_ref[0]
    loss_acc[...] = jnp.zeros_like(loss_acc)
    sums[...] = jnp.zeros_like(sums)

    totals[...] = jnp.zeros_like(totals)
    out[...] = jnp.zeros_like(out)
    for copy in own:
        copy.wait()

    def group(g, _):
        @pl.when(g == 0)
        def _():
            relay(0, passed[0])
            arrived(below, shard_rows, 0)
            arrived(above, shard_rows, 1)
            send(below, first_rows, 3, up_to)
            send(above, second_rows, 4, down_to)
            arrived(cross, shard_rows, 2)
            swap(0, below)
            swap(1, above)
            swap(2, cross)
            relay(passed[0], passed[1])
            arrived(opposite, first_rows, 3)
            arrived(opposite, second_rows, 4)
            send(cross, shard_rows, 5, up_to)
            send(cross, shard_rows, 6, down_to)
            send(opposite, shard_rows, 7, cross_to)
            swap(3, opposite)
            relay(passed[1], passed[2])
            swapped(0, below)
            swapped(1, above)
            swapped(3, opposite)

        @pl.when(g == 1)
        def _():
            relay(passed[3], passed[4])
            arrived(cross_below, shard_rows, 5)
            swap(4, cross_below)
            arrived(cross_above, shard_rows, 6)
            swap(5, cross_above)
            arrived(cross_opposite, shard_rows, 7)
            swap(6, cross_opposite)
            relay(passed[4], passed[5])
            swapped(2, cross)
            swapped(4, cross_below)
            swapped(5, cross_above)
            swapped(6, cross_opposite)

        side = x_hi + g * (1 - 2 * x_hi)
        begin = pl.multiple_of(side * (width // 2), width // 2)

        def embed(kind, _):
            def one(m, total):
                for k in range(STEP):
                    part = pl.ds(pl.multiple_of(begin + (m * STEP + k) * 256, 256), 256)
                    value = dot_t(piece(kind)[...], weights[kind, part, :])
                    emb[kind, :, part] = value
                    square = value * value
                    total = total + square[:, 0:128] + square[:, 128:256]
                return total

            totals[kind] = lax.fori_loop(0, tiles // 2 // STEP, one, totals[kind])
            return 0

        lax.fori_loop(0, 2, embed, 0)

        @pl.when(g == 0)
        def _():
            relay(passed[2], passed[3])

        @pl.when(g == 1)
        def _():
            relay(passed[5], passed[6])


        def through(kind, _):
            half = pl.ds(begin, width // 2)
            hi_half, lo_half = split(emb[1 - kind, :, half])

            def back(part, carry):
                right = weights[kind, half, part]
                out[kind, :, part] += dot(hi_half, right) + dot(lo_half, right)
                return carry

            over_tiles(back, 0)
            return 0

        lax.fori_loop(0, 2, through, 0)
        return 0

    lax.fori_loop(0, 2, group, 0)

    def inv_copy(n, base, to):
        return remote(inv_rows.at[OWN], inv_rows.at[base], inv_send.at[n], inv_recv.at[n], to)

    inv_copies = [
        inv_copy(2, Z1, z1_to),
        inv_copy(3, Z2, far_to),
        inv_copy(0, CORE, core_to),
        inv_copy(1, X_LO, x_to),
    ]

    for kind in range(2):
        inverse = lax.rsqrt(jnp.sum(totals[kind], axis=-1, keepdims=True) + 1e-06)
        wide = jnp.broadcast_to(inverse, (rows, 128))
        inv[kind] = wide
        inv_rows[OWN, kind] = wide.T[0:8]
    for copy in inv_copies:
        copy.start()

    def queries(kind, _):
        factor = inv[1 - kind][:, 0:1]
        for n in range(tiles):
            a_hi[kind, :, tile(n)], a_lo[kind, :, tile(n)] = split(out[kind, :, tile(n)] * factor)
        return 0

    lax.fori_loop(0, 2, queries, 0)

    def coefs(keys, kind, inverses, diagonal):
        keys = keys[...]
        inner = dot_t(a_hi[kind], keys) + dot_t(a_lo[kind], keys)
        factor = scale * inverses
        logit = inner * factor + bias
        row = lax.broadcasted_iota(jnp.int32, logit.shape, 0)
        column = lax.broadcasted_iota(jnp.int32, logit.shape, 1)
        label_rows = jnp.where(diagonal, rows, 0)
        sign = jnp.where((row == column) & (row < label_rows), -1.0, 1.0).astype(jnp.float32)
        signed = sign * logit
        coef = (sign * factor) / (1.0 + jnp.exp(-signed))

        @pl.when(kind == 1)
        def _():
            loss = jnp.maximum(signed, 0.0) + jnp.log1p(jnp.exp(-jnp.abs(signed)))
            loss_acc[...] += loss[:, 0:128] + loss[:, 128:256]

        return split(coef)

    def add_terms(keys, kind, coef_hi, coef_lo):
        def add(part, carry):
            key = keys[:, part]
            sums[kind, :, part] += dot(coef_hi, key) + dot(coef_lo, key)
            return carry

        over_tiles(add, 0)

    def out_of_space(kind):
        for n in range(tiles):
            hi[:, tile(n)], lo[:, tile(n)] = split(sums[kind, :, tile(n)])

        def back(part, radial):
            right = weights[kind, part, :]
            value = dot_t(hi[...], right) + dot_t(lo[...], right)
            out[1 - kind, :, part] = value
            product = value * emb[1 - kind, :, part]
            return radial + product[:, 0:128] + product[:, 128:256]

        radial_sums[...] = over_tiles(back, jnp.zeros((rows, 128), jnp.float32))

    out_refs = (grad_image_ref, grad_text_ref)

    def finish(query):
        inverse = inv[query][:, 0:1]
        radial = jnp.sum(radial_sums[...], axis=-1, keepdims=True)
        factor = inverse * inverse * inverse * radial
        for k in range(2):

            @pl.when(query == k)
            def _(out_ref=out_refs[k]):
                for n in range(tiles):
                    out_ref[:, tile(n)] = (
                        inverse * out[query, :, tile(n)] - factor * emb[query, :, tile(n)]
                    )

    before_finish = 14

    def chunks_by(n):
        middle = jnp.minimum(passed[6] + (n + 1) // 2, before_finish)
        middle = jnp.where(n < 0, passed[6], middle)
        return jnp.where(n < 8, middle, jnp.where(n < 9, 15, PIECES))

    def key_norms(keys, kind):
        def one(part, total):
            value = dot_t(keys[...], weights[kind, part, :])
            square = value * value
            return total + square[:, 0:128] + square[:, 128:256]

        total = over_tiles(one, jnp.zeros((rows, 128), jnp.float32))
        inverse = lax.rsqrt(jnp.sum(total, axis=-1, keepdims=True) + 1e-06)
        key_inv[...] = jnp.broadcast_to(inverse, (rows, 128)).T[0:8]

    def last_inverses():
        for copy in inv_copies[:2]:
            copy.wait_recv()
        for k, block in enumerate((Z1, Z2)):
            key_inv[:, k * part_rows : (k + 1) * part_rows] = inv_rows[
                block, 1, :, rows - part_rows : rows
            ]

    def step(n, _):
        relay(jnp.where(n == 8, before_finish, chunks_by(n - 1)), chunks_by(n))

        @pl.when(n == 2)
        def _():
            for copy in whole[2:] + inv_copies[2:]:
                copy.wait_recv()

        @pl.when(n == 4)
        def _():
            for copy in whole[:2]:
                copy.wait_recv()

        @pl.when(n == 7)
        def _():
            wait_z2(0, CHUNKS)

        @pl.when(n >= 8)
        def _():
            wait_z2(CHUNKS + (n - 8) * per_part, CHUNKS + (n - 7) * per_part)

        kind = jnp.where(n < 6, n % 2, n // 8)
        keys = piece(n)

        @pl.when((n >= 6) & (n < 9))
        def _():
            key_norms(keys, kind)

        @pl.when(n == 9)
        def _():
            last_inverses()

        known = inv_rows[jnp.minimum(n // 2, X_LO), kind, 0:1, :]
        inverses = jnp.where(n < 6, known, key_inv[0:1, :])
        coef_hi, coef_lo = coefs(keys, kind, inverses, n < 2)
        add_terms(keys, kind, coef_hi, coef_lo)
        return 0

    def phase(kind, _):
        lax.fori_loop(8 * kind, 8 + 2 * kind, step, 0)

        @pl.when(kind == 0)
        def _():
            relay(chunks_by(7), before_finish)

        out_of_space(kind)
        finish(1 - kind)
        return 0

    lax.fori_loop(0, 2, phase, 0)
    loss_ref[...] = jnp.sum(loss_acc[...].T, axis=0, keepdims=True) / (5 * rows)

    for copy in whole + inv_copies:
        copy.wait_send()

    def sent(j, _):
        z1_copy(j).wait_send()
        z2_copy(j).wait_send()
        return 0

    lax.fori_loop(0, PIECES, sent, 0)
    for number, to in enumerate(own_targets):
        own_shard_copy(0, number, to).wait_send()
    for slot, part, number in (
        (below, first_rows, 3),
        (above, second_rows, 4),
        (cross, shard_rows, 5),
        (cross, shard_rows, 6),
        (opposite, shard_rows, 7),
    ):
        shard_copy(core, slot, part, number, number, core_to).wait_send()
    for number, slot in enumerate(
        (below, above, cross, opposite, cross_below, cross_above, cross_opposite)
    ):
        shard_copy(core, slot, shard_rows, 8 + number, 8 + number, core_to).wait_send()


def run(skip, image, text, image_w, text_w, scale, bias):
    rows, width = image.shape
    dma = pltpu.SemaphoreType.DMA
    f32, bf16 = jnp.float32, jnp.bfloat16
    any_spec = pl.BlockSpec(memory_space=pl.ANY)
    vmem = pl.BlockSpec(memory_space=pltpu.VMEM)
    smem = pl.BlockSpec(memory_space=pltpu.SMEM)
    grad_image, grad_text, loss = pl.pallas_call(
        functools.partial(kernel, skip),
        out_shape=(
            jax.ShapeDtypeStruct((rows, width), f32),
            jax.ShapeDtypeStruct((rows, width), f32),
            jax.ShapeDtypeStruct((1, rows), f32),
        ),
        in_specs=[any_spec, any_spec, any_spec, any_spec, smem, smem],
        out_specs=(vmem, vmem, vmem),
        scratch_shapes=[
            pltpu.VMEM((10 * rows, width), bf16),
            pltpu.VMEM((2, width, width), bf16),
            pltpu.VMEM((2, rows, width), f32),
            pltpu.VMEM((2, rows, 128), f32),
            pltpu.VMEM((5, 2, 8, rows), f32),
            pltpu.VMEM((2, rows, 128), f32),
            pltpu.VMEM((8, rows), f32),
            pltpu.VMEM((rows, 128), f32),
            pltpu.VMEM((2, rows, width), bf16),
            pltpu.VMEM((2, rows, width), bf16),
            pltpu.VMEM((2, rows, width), f32),
            pltpu.VMEM((rows, width), bf16),
            pltpu.VMEM((rows, width), bf16),
            pltpu.VMEM((rows, 128), f32),
            pltpu.VMEM((2, rows, width), f32),
            dma((4,)),
            dma((4,)),
            dma((4,)),
            dma((2 * CHUNKS,)),
            dma((2 * CHUNKS,)),
            dma((2 * CHUNKS,)),
            dma((2 * CHUNKS,)),
            dma((15,)),
            dma((15,)),
            dma((4,)),
            dma((4,)),
        ],
        compiler_params=pltpu.CompilerParams(
            collective_id=skip, has_side_effects=True, vmem_limit_bytes=48 * 2**20
        ),
    )(image, text, image_w.T, text_w.T, scale, bias)
    return grad_image, grad_text, loss


def body(image, text, image_w, text_w, scale, bias, flags):
    skip = 10 - jnp.sum(flags)
    grad_image, grad_text, loss = lax.switch(
        skip - 1,
        [functools.partial(run, 1), functools.partial(run, 2), functools.partial(run, 3)],
        image,
        text,
        image_w,
        text_w,
        scale,
        bias,
    )
    return grad_image, grad_text, loss.reshape(loss.shape[1])


def solution(mesh):
    placed = (
        P(("dp", "tensor"), None),
        P(("dp", "tensor"), None),
        P(None, "tensor"),
        P(None, "tensor"),
        P(),
        P(),
        P(),
    )
    return jax.shard_map(
        body,
        mesh=mesh,
        in_specs=placed,
        out_specs=(P(("dp", "tensor"), None), P(("dp", "tensor"), None), P(("dp", "tensor"))),
        check_vma=False,
    )
```

```python
import functools

import jax
import jax.numpy as jnp
from jax import lax
from jax.experimental import pallas as pl
from jax.experimental.pallas import tpu as pltpu
from jax.sharding import PartitionSpec as P

MESH = pl.DeviceIdType.MESH
OWN, CORE, X_LO, Z1, Z2 = 0, 1, 2, 3, 4
PARTS = 2
CHUNKS = 8
PIECES = 2 * CHUNKS
STEP = 3
AHEAD = {1: 2, 2: 4, 3: 4}
PASSED = {1: (3, 4, 5, 6, 7, 8, 9), 2: (3, 5, 6, 7, 8, 9, 10), 3: (3, 4, 5, 6, 7, 8, 9)}


def flip(value, bit):
    size = 2**bit
    return value + size * (1 - 2 * ((value // size) % 2))


def dot(first, second):
    return jnp.dot(first, second, preferred_element_type=jnp.float32)


def dot_t(first, second):
    return lax.dot_general(
        first, second, (((1,), (1,)), ((), ())), preferred_element_type=jnp.float32
    )


def split(value):
    high = value.astype(jnp.bfloat16)
    low = (value - high.astype(jnp.float32)).astype(jnp.bfloat16)
    return high, low


def kernel(
    skip,
    image_ref,
    text_ref,
    image_w_ref,
    text_w_ref,
    scale_ref,
    bias_ref,
    grad_image_ref,
    grad_text_ref,
    loss_ref,
    feat,
    weights,
    emb,
    inv,
    inv_rows,
    totals,
    key_inv,
    radial_sums,
    a_hi,
    a_lo,
    sums,
    hi,
    lo,
    loss_acc,
    out,
    own_sem,
    send_sem,
    recv_sem,
    z1_send,
    z1_recv,
    z2_send,
    z2_recv,
    w_send,
    w_recv,
    inv_send,
    inv_recv,
):
    rows, width = image_ref.shape
    shard = image_w_ref.shape[0]
    dp = lax.axis_index("dp")
    tensor = lax.axis_index("tensor")
    core = dp % 2
    y = tensor % 4
    x_hi = tensor // 4

    def at(x_side, y_place):
        return x_side * 4 + (y_place + 4) % 4

    if skip == 1:
        z1_dp, far_dp = flip(dp, 2), flip(dp, 3)
        hop_dp = flip(flip(dp, 2), 3)
    elif skip == 2:
        z1_dp, far_dp = flip(dp, 1), flip(dp, 3)
        hop_dp = flip(flip(dp, 1), 3)
    else:
        z1_dp, far_dp = flip(dp, 1), flip(dp, 2)
        hop_dp = far_dp
    core_to = (flip(dp, 0), tensor)
    x_to = (flip(dp, 4), tensor)
    cross_to = (flip(dp, 4), at(1 - x_hi, y))
    up_to = (dp, at(x_hi, y + 1))
    down_to = (dp, at(x_hi, y - 1))
    z1_to = (z1_dp, tensor)
    hop_to = (hop_dp, tensor)
    far_to = (far_dp, tensor)

    barrier = pltpu.get_barrier_semaphore()
    peers = [core_to, x_to, cross_to, up_to, down_to, z1_to, hop_to]
    if skip != 3:
        peers.append(far_to)
    for peer in peers:
        pl.semaphore_signal(barrier, inc=1, device_id=peer, device_id_type=MESH)
    pl.semaphore_wait(barrier, len(peers))

    def remote(src, dst, send, recv, to):
        return pltpu.make_async_remote_copy(
            src_ref=src, dst_ref=dst, send_sem=send, recv_sem=recv, device_id=to, device_id_type=MESH
        )

    chunk_rows = rows // CHUNKS
    inputs = (image_ref, text_ref)
    def rows_of(j):
        return pl.ds(pl.multiple_of((j % CHUNKS) * chunk_rows, chunk_rows), chunk_rows)

    per_part = CHUNKS // PARTS
    part_rows = rows // PARTS

    def landing(far, j):
        k = j - CHUNKS
        image = (6 + far) * rows + j * chunk_rows
        text = 8 * rows + (2 * (k // per_part) + far) * part_rows
        text = text + (k % per_part) * chunk_rows
        start = jnp.where(j < CHUNKS, image, text)
        return feat.at[pl.ds(pl.multiple_of(start, chunk_rows), chunk_rows)]

    def z1_copy(j, source=None):
        place = landing(0, j)
        return remote(
            place if source is None else source, place, z1_send.at[j], z1_recv.at[j], z1_to
        )

    def z2_copy(j, source=None):
        source = landing(0, j) if source is None else source
        return remote(source, landing(1, j), z2_send.at[j], z2_recv.at[j], hop_to)

    def send_chunk(j, _, source=None):
        source = feat.at[pl.ds(pl.multiple_of(j * chunk_rows, chunk_rows), chunk_rows)] if source is None else source
        z1_copy(j, source).start()
        if skip == 3:
            z2_copy(j, source).start()
        return 0

    ahead = AHEAD[skip]
    passed = PASSED[skip]
    lax.fori_loop(0, ahead, lambda j, _: send_chunk(j, 0, image_ref.at[rows_of(j)]), 0)

    w_inputs = (image_w_ref, text_w_ref)
    shard_rows = (0, shard)
    first_rows = (0, shard // 2)
    second_rows = (shard // 2, shard // 2)
    below, above, opposite = at(x_hi, y - 1), at(x_hi, y + 1), at(x_hi, y + 2)
    cross = at(1 - x_hi, y)
    cross_below, cross_above, cross_opposite = (
        at(1 - x_hi, y - 1),
        at(1 - x_hi, y + 1),
        at(1 - x_hi, y + 2),
    )

    def place(kind, slot, part):
        offset = pl.multiple_of(slot * shard + part[0], shard // 2)
        return weights.at[kind, pl.ds(offset, part[1])]

    def shard_copy(kind, slot, part, send, recv, to):
        ref = place(kind, slot, part)
        return remote(ref, ref, w_send.at[send], w_recv.at[recv], to)

    def own_shard_copy(kind, number, to):
        return remote(
            w_inputs[kind],
            place(kind, tensor, shard_rows),
            w_send.at[number],
            w_recv.at[number],
            to,
        )

    own_targets = (up_to, down_to, cross_to)
    for kind in range(2):

        @pl.when(core == kind)
        def _():
            for number, to in enumerate(own_targets):
                own_shard_copy(kind, number, to).start()

    def piece(n):
        return feat.at[pl.ds(pl.multiple_of(n * rows, rows), rows)]

    def whole_copy(kind, base, n, to):
        return remote(
            inputs[kind], piece(2 * base + kind), send_sem.at[n], recv_sem.at[n], to
        )

    whole = [
        whole_copy(0, X_LO, 2, x_to),
        whole_copy(1, X_LO, 3, x_to),
        whole_copy(0, CORE, 0, core_to),
        whole_copy(1, CORE, 1, core_to),
    ]
    for copy in whole:
        copy.start()
    own = [pltpu.make_async_copy(inputs[k], piece(k), own_sem.at[k]) for k in range(2)]
    for kind in range(2):
        own.append(
            pltpu.make_async_copy(
                w_inputs[kind], place(kind, tensor, shard_rows), own_sem.at[2 + kind]
            )
        )
    for copy in own:
        copy.start()

    def send(slot, part, number, to):
        shard_copy(core, slot, part, number, number, to).start()

    def swap(number, slot):
        send(slot, shard_rows, 8 + number, core_to)

    def arrived(slot, part, recv):
        shard_copy(core, slot, part, recv, recv, core_to).wait_recv()

    def swapped(number, slot):
        shard_copy(1 - core, slot, shard_rows, 8 + number, 8 + number, core_to).wait_recv()

    def relay(first, last):
        def one(j, _):
            z1_copy(j).wait_recv()
            if skip != 3:
                z2_copy(j).start()

            @pl.when(j + ahead < PIECES)
            def _():
                send_chunk(j + ahead, 0)

            return 0

        lax.fori_loop(first, last, one, 0)

    def wait_z2(first, last):
        def one(j, _):
            z2_copy(j).wait_recv()
            return 0

        lax.fori_loop(first, last, one, 0)

    tiles = width // 256

    def tile(n):
        return slice(n * 256, (n + 1) * 256)

    def over_tiles(body, carry):
        def several(m, carry):
            for k in range(STEP):
                carry = body(pl.ds(pl.multiple_of((m * STEP + k) * 256, 256), 256), carry)
            return carry

        return lax.fori_loop(0, tiles // STEP, several, carry)

    scale = scale_ref[0]
    bias = bias_ref[0]
    loss_acc[...] = jnp.zeros_like(loss_acc)
    sums[...] = jnp.zeros_like(sums)

    totals[...] = jnp.zeros_like(totals)
    out[...] = jnp.zeros_like(out)
    for copy in own:
        copy.wait()

    def group(g, _):
        @pl.when(g == 0)
        def _():
            relay(0, passed[0])
            arrived(below, shard_rows, 0)
            arrived(above, shard_rows, 1)
            send(below, first_rows, 3, up_to)
            send(above, second_rows, 4, down_to)
            arrived(cross, shard_rows, 2)
            swap(0, below)
            swap(1, above)
            swap(2, cross)
            relay(passed[0], passed[1])
            arrived(opposite, first_rows, 3)
            arrived(opposite, second_rows, 4)
            send(cross, shard_rows, 5, up_to)
            send(cross, shard_rows, 6, down_to)
            send(opposite, shard_rows, 7, cross_to)
            swap(3, opposite)
            relay(passed[1], passed[2])
            swapped(0, below)
            swapped(1, above)
            swapped(3, opposite)

        @pl.when(g == 1)
        def _():
            relay(passed[3], passed[4])
            arrived(cross_below, shard_rows, 5)
            swap(4, cross_below)
            arrived(cross_above, shard_rows, 6)
            swap(5, cross_above)
            arrived(cross_opposite, shard_rows, 7)
            swap(6, cross_opposite)
            relay(passed[4], passed[5])
            swapped(2, cross)
            swapped(4, cross_below)
            swapped(5, cross_above)
            swapped(6, cross_opposite)

        side = x_hi + g * (1 - 2 * x_hi)
        begin = pl.multiple_of(side * (width // 2), width // 2)

        def embed(kind, _):
            def one(m, total):
                for k in range(STEP):
                    part = pl.ds(pl.multiple_of(begin + (m * STEP + k) * 256, 256), 256)
                    value = dot_t(piece(kind)[...], weights[kind, part, :])
                    emb[kind, :, part] = value
                    square = value * value
                    total = total + square[:, 0:128] + square[:, 128:256]
                return total

            totals[kind] = lax.fori_loop(0, tiles // 2 // STEP, one, totals[kind])
            return 0

        lax.fori_loop(0, 2, embed, 0)

        @pl.when(g == 0)
        def _():
            relay(passed[2], passed[3])

        @pl.when(g == 1)
        def _():
            relay(passed[5], passed[6])


        def through(kind, _):
            half = pl.ds(begin, width // 2)
            hi_half, lo_half = split(emb[1 - kind, :, half])

            def back(part, carry):
                right = weights[kind, half, part]
                out[kind, :, part] += dot(hi_half, right) + dot(lo_half, right)
                return carry

            over_tiles(back, 0)
            return 0

        lax.fori_loop(0, 2, through, 0)
        return 0

    lax.fori_loop(0, 2, group, 0)

    def inv_copy(n, base, to):
        return remote(inv_rows.at[OWN], inv_rows.at[base], inv_send.at[n], inv_recv.at[n], to)

    inv_copies = [
        inv_copy(2, Z1, z1_to),
        inv_copy(3, Z2, far_to),
        inv_copy(0, CORE, core_to),
        inv_copy(1, X_LO, x_to),
    ]

    for kind in range(2):
        inverse = lax.rsqrt(jnp.sum(totals[kind], axis=-1, keepdims=True) + 1e-06)
        wide = jnp.broadcast_to(inverse, (rows, 128))
        inv[kind] = wide
        inv_rows[OWN, kind] = wide.T[0:8]
    for copy in inv_copies:
        copy.start()

    def queries(kind, _):
        factor = inv[1 - kind][:, 0:1]
        for n in range(tiles):
            a_hi[kind, :, tile(n)], a_lo[kind, :, tile(n)] = split(out[kind, :, tile(n)] * factor)
        return 0

    lax.fori_loop(0, 2, queries, 0)

    def coefs(keys, kind, inverses, diagonal):
        keys = keys[...]
        inner = dot_t(a_hi[kind], keys) + dot_t(a_lo[kind], keys)
        factor = scale * inverses
        logit = inner * factor + bias
        row = lax.broadcasted_iota(jnp.int32, logit.shape, 0)
        column = lax.broadcasted_iota(jnp.int32, logit.shape, 1)
        label_rows = jnp.where(diagonal, rows, 0)
        sign = jnp.where((row == column) & (row < label_rows), -1.0, 1.0).astype(jnp.float32)
        signed = sign * logit
        coef = (sign * factor) / (1.0 + jnp.exp(-signed))

        @pl.when(kind == 1)
        def _():
            loss = jnp.maximum(signed, 0.0) + jnp.log1p(jnp.exp(-jnp.abs(signed)))
            loss_acc[...] += loss[:, 0:128] + loss[:, 128:256]

        return split(coef)

    def add_terms(keys, kind, coef_hi, coef_lo):
        def add(part, carry):
            key = keys[:, part]
            sums[kind, :, part] += dot(coef_hi, key) + dot(coef_lo, key)
            return carry

        over_tiles(add, 0)

    def out_of_space(kind):
        for n in range(tiles):
            hi[:, tile(n)], lo[:, tile(n)] = split(sums[kind, :, tile(n)])

        radial = jnp.zeros((rows, 128), jnp.float32)
        for n in range(tiles):
            part = tile(n)
            right = weights[kind, part, :]
            value = dot_t(hi[...], right) + dot_t(lo[...], right)
            out[1 - kind, :, part] = value
            product = value * emb[1 - kind, :, part]
            radial = radial + product[:, 0:128] + product[:, 128:256]
        radial_sums[...] = radial

    out_refs = (grad_image_ref, grad_text_ref)

    def finish(query):
        inverse = inv[query][:, 0:1]
        radial = jnp.sum(radial_sums[...], axis=-1, keepdims=True)
        factor = inverse * inverse * inverse * radial
        for k in range(2):

            @pl.when(query == k)
            def _(out_ref=out_refs[k]):
                for n in range(tiles):
                    out_ref[:, tile(n)] = (
                        inverse * out[query, :, tile(n)] - factor * emb[query, :, tile(n)]
                    )

    before_finish = 14

    def chunks_by(n):
        middle = jnp.minimum(passed[6] + (n + 1) // 2, before_finish)
        middle = jnp.where(n < 0, passed[6], middle)
        return jnp.where(n < 8, middle, jnp.where(n < 9, 15, PIECES))

    def key_norms(keys, kind):
        def one(part, total):
            value = dot_t(keys[...], weights[kind, part, :])
            square = value * value
            return total + square[:, 0:128] + square[:, 128:256]

        total = over_tiles(one, jnp.zeros((rows, 128), jnp.float32))
        inverse = lax.rsqrt(jnp.sum(total, axis=-1, keepdims=True) + 1e-06)
        key_inv[...] = jnp.broadcast_to(inverse, (rows, 128)).T[0:8]

    def last_inverses():
        for copy in inv_copies[:2]:
            copy.wait_recv()
        for k, block in enumerate((Z1, Z2)):
            key_inv[:, k * part_rows : (k + 1) * part_rows] = inv_rows[
                block, 1, :, rows - part_rows : rows
            ]

    def step(n, _):
        relay(jnp.where(n == 8, before_finish, chunks_by(n - 1)), chunks_by(n))

        @pl.when(n == 2)
        def _():
            for copy in whole[2:] + inv_copies[2:]:
                copy.wait_recv()

        @pl.when(n == 4)
        def _():
            for copy in whole[:2]:
                copy.wait_recv()

        @pl.when(n == 7)
        def _():
            wait_z2(0, CHUNKS)

        @pl.when(n >= 8)
        def _():
            wait_z2(CHUNKS + (n - 8) * per_part, CHUNKS + (n - 7) * per_part)

        kind = jnp.where(n < 6, n % 2, n // 8)
        keys = piece(n)

        @pl.when((n >= 6) & (n < 9))
        def _():
            key_norms(keys, kind)

        @pl.when(n == 9)
        def _():
            last_inverses()

        known = inv_rows[jnp.minimum(n // 2, X_LO), kind, 0:1, :]
        inverses = jnp.where(n < 6, known, key_inv[0:1, :])
        coef_hi, coef_lo = coefs(keys, kind, inverses, n < 2)
        add_terms(keys, kind, coef_hi, coef_lo)
        return 0

    def phase(kind, _):
        lax.fori_loop(8 * kind, 8 + 2 * kind, step, 0)

        @pl.when(kind == 0)
        def _():
            relay(chunks_by(7), before_finish)

        out_of_space(kind)
        finish(1 - kind)
        return 0

    lax.fori_loop(0, 2, phase, 0)
    loss_ref[...] = jnp.sum(loss_acc[...].T, axis=0, keepdims=True) / (5 * rows)

    for copy in whole + inv_copies:
        copy.wait_send()

    def sent(j, _):
        z1_copy(j).wait_send()
        z2_copy(j).wait_send()
        return 0

    lax.fori_loop(0, PIECES, sent, 0)
    for number, to in enumerate(own_targets):
        own_shard_copy(0, number, to).wait_send()
    for slot, part, number in (
        (below, first_rows, 3),
        (above, second_rows, 4),
        (cross, shard_rows, 5),
        (cross, shard_rows, 6),
        (opposite, shard_rows, 7),
    ):
        shard_copy(core, slot, part, number, number, core_to).wait_send()
    for number, slot in enumerate(
        (below, above, cross, opposite, cross_below, cross_above, cross_opposite)
    ):
        shard_copy(core, slot, shard_rows, 8 + number, 8 + number, core_to).wait_send()


def run(skip, image, text, image_w, text_w, scale, bias):
    rows, width = image.shape
    dma = pltpu.SemaphoreType.DMA
    f32, bf16 = jnp.float32, jnp.bfloat16
    any_spec = pl.BlockSpec(memory_space=pl.ANY)
    vmem = pl.BlockSpec(memory_space=pltpu.VMEM)
    smem = pl.BlockSpec(memory_space=pltpu.SMEM)
    grad_image, grad_text, loss = pl.pallas_call(
        functools.partial(kernel, skip),
        out_shape=(
            jax.ShapeDtypeStruct((rows, width), f32),
            jax.ShapeDtypeStruct((rows, width), f32),
            jax.ShapeDtypeStruct((1, rows), f32),
        ),
        in_specs=[any_spec, any_spec, any_spec, any_spec, smem, smem],
        out_specs=(vmem, vmem, vmem),
        scratch_shapes=[
            pltpu.VMEM((10 * rows, width), bf16),
            pltpu.VMEM((2, width, width), bf16),
            pltpu.VMEM((2, rows, width), f32),
            pltpu.VMEM((2, rows, 128), f32),
            pltpu.VMEM((5, 2, 8, rows), f32),
            pltpu.VMEM((2, rows, 128), f32),
            pltpu.VMEM((8, rows), f32),
            pltpu.VMEM((rows, 128), f32),
            pltpu.VMEM((2, rows, width), bf16),
            pltpu.VMEM((2, rows, width), bf16),
            pltpu.VMEM((2, rows, width), f32),
            pltpu.VMEM((rows, width), bf16),
            pltpu.VMEM((rows, width), bf16),
            pltpu.VMEM((rows, 128), f32),
            pltpu.VMEM((2, rows, width), f32),
            dma((4,)),
            dma((4,)),
            dma((4,)),
            dma((2 * CHUNKS,)),
            dma((2 * CHUNKS,)),
            dma((2 * CHUNKS,)),
            dma((2 * CHUNKS,)),
            dma((15,)),
            dma((15,)),
            dma((4,)),
            dma((4,)),
        ],
        compiler_params=pltpu.CompilerParams(
            collective_id=skip, has_side_effects=True, vmem_limit_bytes=48 * 2**20
        ),
    )(image, text, image_w.T, text_w.T, scale, bias)
    return grad_image, grad_text, loss


def body(image, text, image_w, text_w, scale, bias, flags):
    skip = 10 - jnp.sum(flags)
    grad_image, grad_text, loss = lax.switch(
        skip - 1,
        [functools.partial(run, 1), functools.partial(run, 2), functools.partial(run, 3)],
        image,
        text,
        image_w,
        text_w,
        scale,
        bias,
    )
    return grad_image, grad_text, loss.reshape(loss.shape[1])


def solution(mesh):
    placed = (
        P(("dp", "tensor"), None),
        P(("dp", "tensor"), None),
        P(None, "tensor"),
        P(None, "tensor"),
        P(),
        P(),
        P(),
    )
    return jax.shard_map(
        body,
        mesh=mesh,
        in_specs=placed,
        out_specs=(P(("dp", "tensor"), None), P(("dp", "tensor"), None), P(("dp", "tensor"))),
        check_vma=False,
    )
```
